32 devices in a mesh: dom: 16 (over z, y, x), grp: 2 (over core).
Axes of the slice: x: 2, y: 2, z: 4, core: 2. Of those that a mesh axis runs over, the one named last changes fastest.
Arguments:
- features: bfloat16 [256, 768], P(('dom', 'grp')), may hold values from -6 to 6
- w_first: bfloat16 [768, 512], replicated, may hold values from -0.21875 to 0.21875
- w_second: bfloat16 [512, 512], replicated, may hold values from -0.25 to 0.25
- relation_table: bfloat16 [1387, 512], replicated, may hold values from -1.5 to 1.5
- heads: int32 [2, 4096], P(None, ('dom', 'grp')), may hold values from 0 to 15
- relations: int32 [2, 4096], P(None, ('dom', 'grp')), may hold values from 0 to 1386
- tails: int32 [2, 4096], P(None, ('dom', 'grp')), may hold values from 0 to 15
- negatives: int32 [2, 512], replicated, may hold values from 0 to 15
- partner: int32 [2, 16], replicated, may hold values from 0 to 15, as said below
Outputs:
- edge_loss: float32 [2, 4096], P(None, ('dom', 'grp'))
- grad_w1: float32 [768, 512], P('grp')
- grad_w2: float32 [512, 512], P('grp')
The draws below stay inside these ranges and needn't reach their ends.
Inputs may be any that keep to these rules, and one draw needn't show every extreme that they name: partner[r, p] = p XOR m_r with one mask m_r of 1 to 15 for each round r, so partitions meet in pairs.
All inputs are finite; a program needn't handle non-finite values.
Results may differ from the reference program's by a relative error of at most 0.0095.
Values may be sent and summed in bfloat16 or wider, within the bound.
No kernel may reach another device: no remote copies, remote signals or barrier semaphores. Data moves between devices by JAX's collectives and lax.ppermute only.
A program may use at most 64 MiB of HBM per device.

```python
import math
import jax
import jax.numpy as jnp
import numpy as np
from jax import lax

D_IN = 768
NREL = 1387
D_HID = 512
D_ENC = 512
NEG = 512
ROUNDS = 2
EDGE_DEV = 128
NPART = 16
GROUP = 2
ENT_PART = 16
ENTITIES = 256
EDGES = 4096


def draw_partner(key, part):
    masks = jax.random.randint(jax.random.fold_in(key, 7), (ROUNDS, 1), 1, NPART)
    base = jnp.arange(NPART, dtype=jnp.int32)[None, :]
    return jnp.bitwise_xor(base, masks.astype(jnp.int32)).astype(jnp.int32)


def plant(values, rng, low, top_value):
    longest = values.shape.index(max(values.shape))
    spots = []
    for shift in (0, 1):
        where = [jax.random.randint(jax.random.fold_in(rng, axis), (), 0, length) for axis, length in enumerate(values.shape)]
        where[longest] = (where[longest] + shift) % values.shape[longest]
        spots.append(tuple(where))
    return values.at[spots[0]].set(low).at[spots[1]].set(top_value)


def levels(rng, extent, pieces, smallest, high):
    def one(position, parts):
        heights = jax.random.uniform(jax.random.fold_in(jax.random.fold_in(rng, 6), position), (parts,), jnp.float32, smallest / len(pieces), high / len(pieces))
        return jnp.repeat(jnp.exp(heights), extent[position] // parts).reshape((-1,) + (1,) * (len(extent) - position - 1))

    gain = one(*pieces[0])
    for cut in pieces[1:]:
        gain = gain * one(*cut)
    return gain


def rank_table(amount, lean):
    loads = [(1 << 20) // math.isqrt(standing ** lean) + 1 for standing in range(1, amount + 1)]
    width = 1 + sum(loads) // (1 << 30)
    return np.cumsum(np.array([max(1, weight // width) for weight in loads]))


def skewed_ids(key, dims, count, slope):
    grid = rank_table(count, slope)
    ticket = jax.random.randint(jax.random.fold_in(key, 1), dims, 0, int(grid[count - 1]))
    standing = jnp.searchsorted(jnp.asarray(grid, jnp.int32), ticket, side="right")
    return jax.random.permutation(jax.random.fold_in(key, 2), count)[standing].astype(jnp.int32)


def gaussian(rng, shape, deviation, limit, split=(), kind=jnp.bfloat16):
    entries = jax.random.normal(rng, shape, jnp.float32) * deviation
    if len(split) > 0:
        entries = levels(rng, shape, split, -0.22, 0.18) * entries
    return jnp.clip(entries, min=-limit, max=limit).astype(kind)


def setup_inputs(seed: int = 0) -> dict:
    splits = jax.random.split(jax.random.key(seed), 10)
    return {
        "features": gaussian(splits[0], (ENTITIES, D_IN), 1.0, 6.0, ((0, 32),)),
        "w_first": gaussian(splits[1], (D_IN, D_HID), D_IN ** -0.5, 0.21875),
        "w_second": gaussian(splits[2], (D_HID, D_ENC), D_HID ** -0.5, 0.25),
        "relation_table": gaussian(splits[3], (NREL, D_ENC), 0.25, 1.5),
        "heads": plant(jax.random.randint(splits[4], (ROUNDS, EDGES), 0, ENT_PART), jax.random.fold_in(splits[4], 1), 0, ENT_PART - 1).astype(jnp.int32),
        "relations": plant(skewed_ids(splits[5], (ROUNDS, EDGES), NREL, 2), jax.random.fold_in(splits[5], 3), 0, NREL - 1).astype(jnp.int32),
        "tails": plant(jax.random.randint(splits[6], (ROUNDS, EDGES), 0, ENT_PART), jax.random.fold_in(splits[6], 1), 0, ENT_PART - 1).astype(jnp.int32),
        "negatives": plant(jax.random.randint(splits[7], (ROUNDS, NEG), 0, ENT_PART), jax.random.fold_in(splits[7], 1), 0, ENT_PART - 1).astype(jnp.int32),
        "partner": draw_partner(jax.random.fold_in(splits[9], 71), 0),
    }


def encode(rows, w_first, w_second):
    pre_act = jnp.dot(rows, w_first, preferred_element_type=jnp.float32)
    hidden = jax.nn.silu(pre_act).astype(jnp.bfloat16)
    encoded = jnp.dot(hidden, w_second, preferred_element_type=jnp.float32).astype(jnp.bfloat16)
    return (pre_act, hidden, encoded)

def backward(rows, pre_act, hidden, grad_rows, w_second):
    term_second = lax.dot_general(hidden, grad_rows, (((0,), (0,)), ((), ())), preferred_element_type=jnp.float32)
    grad_hidden = lax.dot_general(grad_rows, w_second, (((1,), (1,)), ((), ())), preferred_element_type=jnp.float32)
    sigmoid_pre = jax.nn.sigmoid(pre_act)
    silu_slope = sigmoid_pre * (1.0 + pre_act * (1.0 - sigmoid_pre))
    grad_pre = (grad_hidden * silu_slope).astype(jnp.bfloat16)
    term_first = lax.dot_general(rows, grad_pre, (((0,), (0,)), ((), ())), preferred_element_type=jnp.float32)
    return (term_first, term_second)

def score_block(own, other, relation_table, head_ids, relation_ids, tail_ids, negative_ids):
    half_width = own.shape[1] // 2
    head_rows = jnp.take(own, head_ids, axis=0).astype(jnp.float32)
    rel_rows = jnp.take(relation_table, relation_ids, axis=0).astype(jnp.float32)
    tail_rows = jnp.take(other, tail_ids, axis=0).astype(jnp.float32)
    negative_rows = jnp.take(other, negative_ids, axis=0)
    head_real, head_imag = (head_rows[:, :half_width], head_rows[:, half_width:])
    rel_real, rel_imag = (rel_rows[:, :half_width], rel_rows[:, half_width:])
    query = jnp.concatenate([head_real * rel_real - head_imag * rel_imag, head_real * rel_imag + head_imag * rel_real], axis=1).astype(jnp.bfloat16)
    query_wide = query.astype(jnp.float32)
    positive = lax.optimization_barrier(jnp.sum(query_wide * tail_rows, axis=1))
    negative = lax.dot_general(query, negative_rows, (((1,), (1,)), ((), ())), preferred_element_type=jnp.float32)
    edge_loss = jax.nn.softplus(-positive) + lax.optimization_barrier(jnp.sum(jax.nn.softplus(negative), axis=1)) / negative.shape[1]
    weight_neg = (jax.nn.sigmoid(negative) / negative.shape[1]).astype(jnp.bfloat16)
    weight_pos = -jax.nn.sigmoid(-positive)
    grad_query = weight_pos[:, None] * tail_rows + jnp.dot(weight_neg, negative_rows, preferred_element_type=jnp.float32)
    grad_tail = weight_pos[:, None] * query_wide
    grad_negative = lax.dot_general(weight_neg, query, (((0,), (0,)), ((), ())), preferred_element_type=jnp.float32)
    grad_real, grad_imag = (grad_query[:, :half_width], grad_query[:, half_width:])
    grad_head = jnp.concatenate([grad_real * rel_real + grad_imag * rel_imag, grad_imag * rel_real - grad_real * rel_imag], axis=1)
    row_count = own.shape[0]
    own_part = jax.ops.segment_sum(grad_head, head_ids, num_segments=row_count)
    far_part = jax.ops.segment_sum(grad_tail, tail_ids, num_segments=row_count) + jax.ops.segment_sum(grad_negative, negative_ids, num_segments=row_count)
    return (edge_loss, own_part, far_part)

def take_rows(table, part_index, row_count):
    start = (part_index * row_count).astype(jnp.int32)
    return lax.dynamic_slice_in_dim(table, start, row_count, 0)

def group_total(partials):
    narrow = lax.optimization_barrier(partials.astype(jnp.bfloat16))
    return lax.optimization_barrier(jnp.sum(narrow.astype(jnp.float32), axis=0)).astype(jnp.bfloat16)

def reference(features, w_first, w_second, relation_table, heads, relations, tails, negatives, partner):
    pre_act, hidden, encoded = encode(features, w_first, w_second)
    part_count = partner.shape[1]
    row_count = encoded.shape[0] // part_count
    edge_span = heads.shape[1] // part_count
    zero_first = jnp.zeros(w_first.shape, jnp.float32)
    zero_second = jnp.zeros(w_second.shape, jnp.float32)

    def one_partition(totals, part_index):
        total_first, total_second = totals
        own = take_rows(encoded, part_index, row_count)
        own_acc = jnp.zeros((GROUP, row_count, encoded.shape[1]), jnp.float32)
        round_losses = []
        for bucket in range(ROUNDS):
            partner_index = partner[bucket, part_index]
            other = take_rows(encoded, partner_index, row_count)

            def member_ids(table):
                return take_rows(table[bucket], part_index, edge_span).reshape(GROUP, EDGE_DEV)

            def member(edge_tuple):
                return score_block(own, other, relation_table, edge_tuple[0], edge_tuple[1], edge_tuple[2], negatives[bucket])
            edge_loss, own_part, far_part = lax.map(member, (member_ids(heads), member_ids(relations), member_ids(tails)))
            round_losses.append(edge_loss.reshape(edge_span))
            own_acc = own_acc + own_part
            far_grad = group_total(far_part)
            term_first, term_second = backward(take_rows(features, partner_index, row_count), take_rows(pre_act, partner_index, row_count), take_rows(hidden, partner_index, row_count), far_grad, w_second)
            total_first = total_first + term_first
            total_second = total_second + term_second
        own_grad = group_total(own_acc)
        term_first, term_second = backward(take_rows(features, part_index, row_count), take_rows(pre_act, part_index, row_count), take_rows(hidden, part_index, row_count), own_grad, w_second)
        return ((total_first + term_first, total_second + term_second), jnp.stack(round_losses))
    totals, losses = lax.scan(one_partition, (zero_first, zero_second), jnp.arange(part_count, dtype=jnp.int32))
    total_first, total_second = totals
    edge_loss = jnp.transpose(losses, (1, 0, 2)).reshape(ROUNDS, heads.shape[1])
    squares = jnp.sum(total_first * total_first) + jnp.sum(total_second * total_second)
    factor = jnp.minimum(1.0, math.sqrt(w_first.size + w_second.size) / jnp.sqrt(squares + 1e-06))
    return (edge_loss, total_first * factor, total_second * factor)
```

```python
import functools
import math

import jax
import jax.numpy as jnp
from jax import lax
from jax.experimental import pallas as pl
from jax.experimental.pallas import tpu as pltpu
from jax.sharding import PartitionSpec as P

LANES = 128
F32 = jnp.float32
BF16 = jnp.bfloat16


def partner_2(value, axis, distance):
    return lax.ppermute(value, axis, [(i, i ^ 1 << distance) for i in range(lax.axis_size(axis))])


def encode(rows, w_first, w_second):
    pre_act = jnp.dot(rows, w_first, preferred_element_type=jnp.float32)
    hidden = jax.nn.silu(pre_act).astype(jnp.bfloat16)
    encoded = jnp.dot(hidden, w_second, preferred_element_type=jnp.float32).astype(jnp.bfloat16)
    return (pre_act, hidden, encoded)


def backward(rows, pre_act, hidden, grad_rows, w_second):
    term_second = lax.dot_general(
        hidden, grad_rows, (((0,), (0,)), ((), ())), preferred_element_type=jnp.float32
    )
    grad_hidden = lax.dot_general(
        grad_rows, w_second, (((1,), (1,)), ((), ())), preferred_element_type=jnp.float32
    )
    sigmoid_pre = jax.nn.sigmoid(pre_act)
    silu_slope = sigmoid_pre * (1.0 + pre_act * (1.0 - sigmoid_pre))
    grad_pre = (grad_hidden * silu_slope).astype(jnp.bfloat16)
    term_first = lax.dot_general(
        rows, grad_pre, (((0,), (0,)), ((), ())), preferred_element_type=jnp.float32
    )
    return (term_first, term_second)


def row_select(ids, row_count):
    return ids[:, None] == jnp.arange(row_count, dtype=jnp.int32)[None, :]


def pick_rows(selector, table):
    return jnp.dot(selector.astype(jnp.bfloat16), table, preferred_element_type=jnp.float32)


def add_into_rows(selector, values):
    return lax.dot_general(
        selector.astype(jnp.float32),
        values,
        (((0,), (0,)), ((), ())),
        precision=lax.Precision.HIGHEST,
        preferred_element_type=jnp.float32,
    )


def score_block(own, other, relation_table, head_ids, relation_ids, tail_ids, negative_ids):
    half_width = own.shape[1] // 2
    row_count = own.shape[0]
    head_select = row_select(head_ids, row_count)
    tail_select = row_select(tail_ids, row_count)
    negative_select = row_select(negative_ids, row_count)
    head_rows = pick_rows(head_select, own)
    rel_rows = jnp.take(relation_table, relation_ids, axis=0).astype(jnp.float32)
    tail_rows = pick_rows(tail_select, other)
    negative_rows = pick_rows(negative_select, other).astype(jnp.bfloat16)
    head_real, head_imag = (head_rows[:, :half_width], head_rows[:, half_width:])
    rel_real, rel_imag = (rel_rows[:, :half_width], rel_rows[:, half_width:])
    query = jnp.concatenate(
        [head_real * rel_real - head_imag * rel_imag, head_real * rel_imag + head_imag * rel_real],
        axis=1,
    ).astype(jnp.bfloat16)
    query_wide = query.astype(jnp.float32)
    positive = jnp.sum(query_wide * tail_rows, axis=1)
    negative = lax.dot_general(
        query, negative_rows, (((1,), (1,)), ((), ())), preferred_element_type=jnp.float32
    )
    edge_loss = (
        jax.nn.softplus(-positive) + jnp.sum(jax.nn.softplus(negative), axis=1) / negative.shape[1]
    )
    weight_neg = (jax.nn.sigmoid(negative) / negative.shape[1]).astype(jnp.bfloat16)
    weight_pos = -jax.nn.sigmoid(-positive)
    grad_query = weight_pos[:, None] * tail_rows + jnp.dot(
        weight_neg, negative_rows, preferred_element_type=jnp.float32
    )
    grad_tail = weight_pos[:, None] * query_wide
    grad_negative = lax.dot_general(
        weight_neg, query, (((0,), (0,)), ((), ())), preferred_element_type=jnp.float32
    )
    grad_real, grad_imag = (grad_query[:, :half_width], grad_query[:, half_width:])
    grad_head = jnp.concatenate(
        [grad_real * rel_real + grad_imag * rel_imag, grad_imag * rel_real - grad_real * rel_imag],
        axis=1,
    )
    own_part = add_into_rows(head_select, grad_head)
    far_part = add_into_rows(tail_select, grad_tail) + add_into_rows(negative_select, grad_negative)
    return (edge_loss, own_part, far_part)


def route_rows(payload, xor_mask, bit_count, mover):
    for bit_level in range(bit_count):
        swapped = mover(payload, bit_level)
        payload = jnp.where(xor_mask >> bit_level & 1 == 1, swapped, payload)
    return payload


def spread(
    features, w_first, w_second, relation_table, heads, relations, tails, negatives, partner
):
    pre_act, hidden, encoded = encode(features, w_first, w_second)
    own_block = lax.all_gather(encoded, "grp", axis=0, tiled=True)
    bit_count = lax.axis_size("dom").bit_length() - 1
    total_first = jnp.zeros(w_first.shape, jnp.float32)
    total_second = jnp.zeros(w_second.shape, jnp.float32)
    own_acc = jnp.zeros(own_block.shape, jnp.float32)
    losses = []
    for bucket in range(heads.shape[0]):
        xor_mask = partner[bucket, 0]
        arrived = route_rows(
            encoded,
            xor_mask,
            bit_count,
            lambda payload, bit_level: partner_2(payload, "dom", bit_level),
        )
        far_block = lax.all_gather(arrived, "grp", axis=0, tiled=True)
        edge_loss, own_part, far_part = score_block(
            own_block,
            far_block,
            relation_table,
            heads[bucket],
            relations[bucket],
            tails[bucket],
            negatives[bucket],
        )
        losses.append(edge_loss)
        own_acc = own_acc + own_part
        far_grad = lax.psum_scatter(
            far_part.astype(jnp.bfloat16), "grp", scatter_dimension=0, tiled=True
        )
        returned = route_rows(
            far_grad,
            xor_mask,
            bit_count,
            lambda payload, bit_level: partner_2(payload, "dom", bit_level),
        )
        term_first, term_second = backward(features, pre_act, hidden, returned, w_second)
        total_first = total_first + term_first
        total_second = total_second + term_second
    own_grad = lax.psum_scatter(
        own_acc.astype(jnp.bfloat16), "grp", scatter_dimension=0, tiled=True
    )
    term_first, term_second = backward(features, pre_act, hidden, own_grad, w_second)
    total_first = total_first + term_first
    total_second = total_second + term_second
    part_first, part_second = (
        lax.psum_scatter(
            total_first.astype(jnp.bfloat16), "grp", scatter_dimension=0, tiled=True
        ).astype(jnp.float32),
        lax.psum_scatter(
            total_second.astype(jnp.bfloat16), "grp", scatter_dimension=0, tiled=True
        ).astype(jnp.float32),
    )
    summed_first, summed_second = lax.psum((part_first, part_second), "dom")
    local_squares = jnp.sum(summed_first * summed_first) + jnp.sum(summed_second * summed_second)
    squares = lax.psum(local_squares, "grp")
    factor = jnp.minimum(1.0, math.sqrt(w_first.size + w_second.size) / jnp.sqrt(squares + 1e-06))
    return (jnp.stack(losses), summed_first * factor, summed_second * factor)


def swap(value, axes, distance):
    size = math.prod(lax.axis_size(axis) for axis in axes)
    return lax.ppermute(value, axes, [(i, i ^ distance) for i in range(size)])


def gather_relative(value, axis, bits_at_once):
    rows = value.shape[0]
    order = [0]
    distance = lax.axis_size(axis)
    while distance > 1:
        radix = min(bits_at_once, distance)
        distance //= radix
        moved = [i * distance for i in range(1, radix)]
        arrived = [swap(value, (axis,), step) for step in reversed(moved)][::-1]
        value = jnp.concatenate([value] + arrived, axis=0)
        order = order + [place ^ step for step in moved for place in order]
    assert value.shape[0] == rows * len(order)
    return value, order


def first_above(counts):
    return [sum(counts[:i]) for i in range(len(counts))]


def sigmoid_parts(value):
    small = jnp.exp(-jnp.abs(value))
    softplus = jnp.maximum(value, 0.0) + jnp.log(1.0 + small)
    sigmoid = jnp.where(value >= 0.0, 1.0, small) / (1.0 + small)
    return softplus, sigmoid


def score_kernel(
    sizes,
    order,
    scalars,
    mine,
    other,
    w_first,
    w_second,
    table,
    negatives,
    grad_out,
    loss_out,
    slope_out,
    hidden_out,
    encoded,
    ids,
    grads,
):
    width, rows, rounds, edges = sizes
    group_rows = 2 * rows
    half = encoded.shape[1] // 2
    places = len(order)
    all_rows = places * rows
    me = scalars[0]
    mask = scalars[1]

    features = jnp.concatenate([mine[:, :width], other[:, :width]], axis=0)
    pre_act = jnp.dot(features, w_first[...], preferred_element_type=F32)
    gate = 1.0 / (1.0 + jnp.exp(-pre_act))
    hidden = (pre_act * gate).astype(BF16)
    slope_out[...] = gate * (1.0 + pre_act * (1.0 - gate))
    hidden_out[...] = hidden
    encoded[...] = jnp.dot(hidden, w_second[...], preferred_element_type=F32).astype(BF16).astype(F32)
    ids[:all_rows, :] = mine[:, width:].astype(F32)
    ids[all_rows:, :] = other[:, width:].astype(F32)
    grads[...] = jnp.zeros(grads.shape, F32)

    labels = [((i ^ (me * rows)).astype(F32)) for i in range(group_rows)]
    label_column = (
        lax.broadcasted_iota(jnp.int32, (group_rows, 1), 0) ^ (me * rows)
    )
    drawn = negatives[pl.ds(me, 1), :]
    counts = jnp.sum((drawn == label_column).astype(F32), axis=1, keepdims=True)
    negative_count = negatives.shape[1]
    label_column = label_column.astype(F32)
    low_column = lax.broadcasted_iota(jnp.int32, (LANES, 1), 0).astype(F32)
    blocks = table.shape[1] // LANES
    members = (0, all_rows)

    def id_row(kind, place):
        return jnp.concatenate(
            [ids[pl.ds(base + place * rows + kind * rounds + me, 1), :] for base in members], axis=1
        )

    def pair_rows(place):
        return jnp.concatenate(
            [encoded[pl.ds(pl.multiple_of(base + place * rows, rows), rows), :] for base in members],
            axis=0,
        )

    for spot in range(places):
        key = order[spot]
        far = spot_of(order, key, mask)
        low = id_row(3, spot)
        high = id_row(2, spot)
        low_hot = (low == low_column).astype(BF16)
        hot = jnp.concatenate(
            [low_hot * (high == float(block)).astype(BF16) for block in range(blocks)], axis=0
        )
        relation = jnp.dot(table[...], hot, preferred_element_type=F32).astype(BF16)
        near_rows, far_rows = pair_rows(spot), pair_rows(far)
        near_re, near_im = near_rows[:, :half], near_rows[:, half:]
        far_re, far_im = far_rows[:, :half], far_rows[:, half:]
        pairs = jnp.concatenate(
            [
                jnp.concatenate(
                    [
                        near_re[i : i + 1] * far_re + near_im[i : i + 1] * far_im,
                        near_re[i : i + 1] * far_im - near_im[i : i + 1] * far_re,
                    ],
                    axis=1,
                ).astype(BF16)
                for i in range(group_rows)
            ],
            axis=0,
        )
        scores = jnp.dot(pairs, relation, preferred_element_type=F32)
        head = id_row(0, spot)
        tail = id_row(1, spot)
        negative = jnp.zeros((group_rows, scores.shape[1]), F32)
        for i in range(group_rows):
            negative = jnp.where(
                head == labels[i], scores[i * group_rows : (i + 1) * group_rows], negative
            )
        is_tail = tail == label_column
        positive = jnp.sum(jnp.where(is_tail, negative, 0.0), axis=0, keepdims=True)
        loss, chance = sigmoid_parts(negative)
        loss_positive, chance_positive = sigmoid_parts(-positive)
        if spot == 0:
            loss_out[...] = loss_positive + jnp.sum(loss * counts, axis=0, keepdims=True) / negative_count
        weight = (chance / negative_count).astype(BF16).astype(F32) * counts
        weight = (weight - jnp.where(is_tail, chance_positive, 0.0)).astype(BF16)
        weights = jnp.concatenate(
            [weight * (head == labels[i]).astype(BF16) for i in range(group_rows)], axis=0
        )
        moved = lax.dot_general(
            weights, relation, (((1,), (1,)), ((), ())), preferred_element_type=F32
        )
        far_grad_re = jnp.zeros((group_rows, half), F32)
        far_grad_im = jnp.zeros((group_rows, half), F32)
        near_grad = []
        for i in range(group_rows):
            part_re = moved[i * group_rows : (i + 1) * group_rows, :half]
            part_im = moved[i * group_rows : (i + 1) * group_rows, half:]
            row_re, row_im = near_re[i : i + 1], near_im[i : i + 1]
            far_grad_re = far_grad_re + (row_re * part_re - row_im * part_im)
            far_grad_im = far_grad_im + (row_re * part_im + row_im * part_re)
            near_grad.append(
                jnp.concatenate(
                    [
                        jnp.sum(far_re * part_re + far_im * part_im, axis=0, keepdims=True),
                        jnp.sum(far_im * part_re - far_re * part_im, axis=0, keepdims=True),
                    ],
                    axis=1,
                )
            )
        near_grad = jnp.concatenate(near_grad, axis=0)
        far_grad = jnp.concatenate([far_grad_re, far_grad_im], axis=1)
        for member, base in enumerate(members):
            span = slice(member * rows, (member + 1) * rows)
            near_at = pl.ds(base + spot * rows, rows)
            far_at = pl.ds(pl.multiple_of(base + far * rows, rows), rows)
            grads[near_at, :] = grads[near_at, :] + near_grad[span]
            grads[far_at, :] = grads[far_at, :] + far_grad[span]
    grad_out[...] = grads[...].astype(BF16)


def spot_of(order, key, mask):
    spot_by_key = {value: spot for spot, value in enumerate(order)}
    place = jnp.int32(spot_by_key[key])
    bit = 1
    while bit < len(order):
        place = place ^ jnp.where((mask & bit) != 0, spot_by_key[bit], 0)
        bit *= 2
    return place


def total_kernel(
    limit,
    width,
    scalars,
    mine,
    other,
    grad_mine,
    grad_other,
    slope,
    hidden,
    w_second,
    loss_mine,
    loss_other,
    loss_out,
    first_out,
    second_out,
    first,
    second,
):
    me = scalars[0]
    all_rows = mine.shape[0]
    grad = jnp.concatenate(
        [
            grad_mine[:all_rows].astype(F32) + grad_other[all_rows:].astype(F32),
            grad_mine[all_rows:].astype(F32) + grad_other[:all_rows].astype(F32),
        ],
        axis=0,
    ).astype(BF16)
    across = (((0,), (0,)), ((), ()))
    total_second = lax.dot_general(hidden[...], grad, across, preferred_element_type=F32)
    grad_hidden = lax.dot_general(
        grad, w_second[...], (((1,), (1,)), ((), ())), preferred_element_type=F32
    )
    grad_pre = (grad_hidden * slope[...]).astype(BF16)
    features = jnp.concatenate([mine[:, :width], other[:, :width]], axis=0)
    total_first = lax.dot_general(features, grad_pre, across, preferred_element_type=F32)
    squares = jnp.sum(total_first * total_first, axis=(0, 1), keepdims=True) + jnp.sum(
        total_second * total_second, axis=(0, 1), keepdims=True
    )
    factor = jnp.minimum(1.0, limit / jnp.sqrt(squares + 1e-06))
    first[...] = total_first
    second[...] = total_second
    for source, target in ((first, first_out), (second, second_out)):
        share = target.shape[0]
        target[...] = source[pl.ds(pl.multiple_of(me * share, share), share), :] * factor
    edges = loss_out.shape[1]
    for member in range(2):
        loss_out[pl.ds(member, 1), :] = jnp.where(
            me == member, loss_mine[:, :edges], loss_other[:, edges:]
        )


def together(
    features, w_first, w_second, relation_table, heads, relations, tails, negatives, partner
):
    rows, width = features.shape
    rounds, edges = heads.shape
    hidden_width, encoded_width = w_second.shape
    relation_count = relation_table.shape[0]
    id_rows = jnp.concatenate([heads, tails, relations // LANES, relations % LANES], axis=0)
    payload = jnp.concatenate([features, id_rows.astype(BF16)], axis=1)
    table = jnp.pad(relation_table.T, ((0, 0), (0, -relation_count % LANES)))
    me = lax.axis_index("grp").astype(jnp.int32)
    mask = lax.dynamic_index_in_dim(partner[:, 0], me, keepdims=False) ^ 0
    scalars = jnp.stack([me, mask])
    mine, order = gather_relative(payload, "dom", 4)
    other = swap(mine, ("grp",), 1)
    all_rows = 2 * mine.shape[0]

    vmem = pl.BlockSpec(memory_space=pltpu.VMEM)
    smem = pl.BlockSpec(memory_space=pltpu.SMEM)
    grad, loss, slope, hidden = pl.pallas_call(
        functools.partial(score_kernel, (width, rows, rounds, edges), order),
        out_shape=(
            jax.ShapeDtypeStruct((all_rows, encoded_width), BF16),
            jax.ShapeDtypeStruct((1, 2 * edges), F32),
            jax.ShapeDtypeStruct((all_rows, hidden_width), F32),
            jax.ShapeDtypeStruct((all_rows, hidden_width), BF16),
        ),
        in_specs=[smem] + [vmem] * 6,
        out_specs=(vmem,) * 4,
        scratch_shapes=[
            pltpu.VMEM((all_rows, encoded_width), F32),
            pltpu.VMEM((all_rows, edges), F32),
            pltpu.VMEM((all_rows, encoded_width), F32),
        ],
        compiler_params=pltpu.CompilerParams(vmem_limit_bytes=24 * 1024 * 1024),
        name="scores",
    )(scalars, mine, other, w_first, w_second, table, negatives)
    grad_other = swap(grad, ("grp",), 1)
    loss_other = swap(loss, ("grp",), 1)
    limit = math.sqrt(w_first.size + w_second.size)
    return pl.pallas_call(
        functools.partial(total_kernel, limit, width),
        out_shape=(
            jax.ShapeDtypeStruct((rounds, edges), F32),
            jax.ShapeDtypeStruct((w_first.shape[0] // 2, w_first.shape[1]), F32),
            jax.ShapeDtypeStruct((w_second.shape[0] // 2, w_second.shape[1]), F32),
        ),
        in_specs=[smem] + [vmem] * 9,
        out_specs=(vmem,) * 3,
        scratch_shapes=[pltpu.VMEM(w_first.shape, F32), pltpu.VMEM(w_second.shape, F32)],
        compiler_params=pltpu.CompilerParams(vmem_limit_bytes=24 * 1024 * 1024),
        name="totals",
    )(scalars, mine, other, grad, grad_other, slope, hidden, w_second, loss, loss_other)


def solution(mesh):
    def per_device(features, w_first, w_second, relation_table, heads, relations, tails, *rest):
        rounds, edges = heads.shape
        rows = features.shape[0]
        fits = mesh.shape["grp"] == rounds == 2 and edges == LANES and 4 * rounds == rows
        plan = together if fits else spread
        return plan(features, w_first, w_second, relation_table, heads, relations, tails, *rest)

    return jax.shard_map(
        per_device,
        mesh=mesh,
        in_specs=(
            P(("dom", "grp"), None),
            P(),
            P(),
            P(),
            P(None, ("dom", "grp")),
            P(None, ("dom", "grp")),
            P(None, ("dom", "grp")),
            P(),
            P(),
        ),
        out_specs=(P(None, ("dom", "grp")), P("grp", None), P("grp", None)),
        check_vma=False,
    )
```

```python
import functools
import math

import jax
import jax.numpy as jnp
from jax import lax
from jax.experimental import pallas as pl
from jax.experimental.pallas import tpu as pltpu
from jax.sharding import PartitionSpec as P

LANES = 128
F32 = jnp.float32
BF16 = jnp.bfloat16


def partner_2(value, axis, distance):
    return lax.ppermute(value, axis, [(i, i ^ 1 << distance) for i in range(lax.axis_size(axis))])


def encode(rows, w_first, w_second):
    pre_act = jnp.dot(rows, w_first, preferred_element_type=jnp.float32)
    hidden = jax.nn.silu(pre_act).astype(jnp.bfloat16)
    encoded = jnp.dot(hidden, w_second, preferred_element_type=jnp.float32).astype(jnp.bfloat16)
    return (pre_act, hidden, encoded)


def backward(rows, pre_act, hidden, grad_rows, w_second):
    term_second = lax.dot_general(
        hidden, grad_rows, (((0,), (0,)), ((), ())), preferred_element_type=jnp.float32
    )
    grad_hidden = lax.dot_general(
        grad_rows, w_second, (((1,), (1,)), ((), ())), preferred_element_type=jnp.float32
    )
    sigmoid_pre = jax.nn.sigmoid(pre_act)
    silu_slope = sigmoid_pre * (1.0 + pre_act * (1.0 - sigmoid_pre))
    grad_pre = (grad_hidden * silu_slope).astype(jnp.bfloat16)
    term_first = lax.dot_general(
        rows, grad_pre, (((0,), (0,)), ((), ())), preferred_element_type=jnp.float32
    )
    return (term_first, term_second)


def row_select(ids, row_count):
    return ids[:, None] == jnp.arange(row_count, dtype=jnp.int32)[None, :]


def pick_rows(selector, table):
    return jnp.dot(selector.astype(jnp.bfloat16), table, preferred_element_type=jnp.float32)


def add_into_rows(selector, values):
    return lax.dot_general(
        selector.astype(jnp.float32),
        values,
        (((0,), (0,)), ((), ())),
        precision=lax.Precision.HIGHEST,
        preferred_element_type=jnp.float32,
    )


def score_block(own, other, relation_table, head_ids, relation_ids, tail_ids, negative_ids):
    half_width = own.shape[1] // 2
    row_count = own.shape[0]
    head_select = row_select(head_ids, row_count)
    tail_select = row_select(tail_ids, row_count)
    negative_select = row_select(negative_ids, row_count)
    head_rows = pick_rows(head_select, own)
    rel_rows = jnp.take(relation_table, relation_ids, axis=0).astype(jnp.float32)
    tail_rows = pick_rows(tail_select, other)
    negative_rows = pick_rows(negative_select, other).astype(jnp.bfloat16)
    head_real, head_imag = (head_rows[:, :half_width], head_rows[:, half_width:])
    rel_real, rel_imag = (rel_rows[:, :half_width], rel_rows[:, half_width:])
    query = jnp.concatenate(
        [head_real * rel_real - head_imag * rel_imag, head_real * rel_imag + head_imag * rel_real],
        axis=1,
    ).astype(jnp.bfloat16)
    query_wide = query.astype(jnp.float32)
    positive = jnp.sum(query_wide * tail_rows, axis=1)
    negative = lax.dot_general(
        query, negative_rows, (((1,), (1,)), ((), ())), preferred_element_type=jnp.float32
    )
    edge_loss = (
        jax.nn.softplus(-positive) + jnp.sum(jax.nn.softplus(negative), axis=1) / negative.shape[1]
    )
    weight_neg = (jax.nn.sigmoid(negative) / negative.shape[1]).astype(jnp.bfloat16)
    weight_pos = -jax.nn.sigmoid(-positive)
    grad_query = weight_pos[:, None] * tail_rows + jnp.dot(
        weight_neg, negative_rows, preferred_element_type=jnp.float32
    )
    grad_tail = weight_pos[:, None] * query_wide
    grad_negative = lax.dot_general(
        weight_neg, query, (((0,), (0,)), ((), ())), preferred_element_type=jnp.float32
    )
    grad_real, grad_imag = (grad_query[:, :half_width], grad_query[:, half_width:])
    grad_head = jnp.concatenate(
        [grad_real * rel_real + grad_imag * rel_imag, grad_imag * rel_real - grad_real * rel_imag],
        axis=1,
    )
    own_part = add_into_rows(head_select, grad_head)
    far_part = add_into_rows(tail_select, grad_tail) + add_into_rows(negative_select, grad_negative)
    return (edge_loss, own_part, far_part)


def route_rows(payload, xor_mask, bit_count, mover):
    for bit_level in range(bit_count):
        swapped = mover(payload, bit_level)
        payload = jnp.where(xor_mask >> bit_level & 1 == 1, swapped, payload)
    return payload


def spread(
    features, w_first, w_second, relation_table, heads, relations, tails, negatives, partner
):
    pre_act, hidden, encoded = encode(features, w_first, w_second)
    own_block = lax.all_gather(encoded, "grp", axis=0, tiled=True)
    bit_count = lax.axis_size("dom").bit_length() - 1
    total_first = jnp.zeros(w_first.shape, jnp.float32)
    total_second = jnp.zeros(w_second.shape, jnp.float32)
    own_acc = jnp.zeros(own_block.shape, jnp.float32)
    losses = []
    for bucket in range(heads.shape[0]):
        xor_mask = partner[bucket, 0]
        arrived = route_rows(
            encoded,
            xor_mask,
            bit_count,
            lambda payload, bit_level: partner_2(payload, "dom", bit_level),
        )
        far_block = lax.all_gather(arrived, "grp", axis=0, tiled=True)
        edge_loss, own_part, far_part = score_block(
            own_block,
            far_block,
            relation_table,
            heads[bucket],
            relations[bucket],
            tails[bucket],
            negatives[bucket],
        )
        losses.append(edge_loss)
        own_acc = own_acc + own_part
        far_grad = lax.psum_scatter(
            far_part.astype(jnp.bfloat16), "grp", scatter_dimension=0, tiled=True
        )
        returned = route_rows(
            far_grad,
            xor_mask,
            bit_count,
            lambda payload, bit_level: partner_2(payload, "dom", bit_level),
        )
        term_first, term_second = backward(features, pre_act, hidden, returned, w_second)
        total_first = total_first + term_first
        total_second = total_second + term_second
    own_grad = lax.psum_scatter(
        own_acc.astype(jnp.bfloat16), "grp", scatter_dimension=0, tiled=True
    )
    term_first, term_second = backward(features, pre_act, hidden, own_grad, w_second)
    total_first = total_first + term_first
    total_second = total_second + term_second
    part_first, part_second = (
        lax.psum_scatter(
            total_first.astype(jnp.bfloat16), "grp", scatter_dimension=0, tiled=True
        ).astype(jnp.float32),
        lax.psum_scatter(
            total_second.astype(jnp.bfloat16), "grp", scatter_dimension=0, tiled=True
        ).astype(jnp.float32),
    )
    summed_first, summed_second = lax.psum((part_first, part_second), "dom")
    local_squares = jnp.sum(summed_first * summed_first) + jnp.sum(summed_second * summed_second)
    squares = lax.psum(local_squares, "grp")
    factor = jnp.minimum(1.0, math.sqrt(w_first.size + w_second.size) / jnp.sqrt(squares + 1e-06))
    return (jnp.stack(losses), summed_first * factor, summed_second * factor)


ROUNDS = 2
HEAD, TAIL, HIGH, LOW = 0, 1, 2, 3


def swap(value, axis, distance):
    return lax.ppermute(value, axis, [(i, i ^ distance) for i in range(lax.axis_size(axis))])


def distances_of(size):
    steps = []
    while size > 4:
        size //= 2
        steps.append([size])
    return steps + [list(range(size - 1, 0, -1))]


def join(value, axis, step, beside=None):
    arrived = [swap(value, axis, distance) for distance in step]
    if beside is not None:
        *arrived, beside = lax.optimization_barrier((*arrived[::-1], beside))
        arrived = arrived[::-1]
    return jnp.concatenate([value] + arrived, axis=0), beside


def keys_of(size):
    keys = [0]
    for step in distances_of(size):
        keys = keys + [key ^ distance for distance in step for key in keys]
    return keys


def place_of(mask, keys):
    place, bit = jnp.int32(0), 1
    while bit < len(keys):
        place = place ^ jnp.where((mask & bit) != 0, keys.index(bit), 0)
        bit *= 2
    return place


def id_row(ids, kind, place, me, rows):
    return ids[pl.ds(place * rows + kind * ROUNDS + me, 1), :]


def pick_relations(ids, places, me, rows, table, picked):
    low_column = lax.broadcasted_iota(jnp.int32, (LANES, 1), 0).astype(F32)
    for first in range(places.start, places.stop, 2):
        low, high = [
            jnp.concatenate([id_row(ids, kind, place, me, rows) for place in (first, first + 1)], axis=1)
            for kind in (LOW, HIGH)
        ]
        low_hot = (low == low_column).astype(BF16)
        hot = jnp.concatenate(
            [low_hot * (high == float(block)).astype(BF16) for block in range(table.shape[1] // LANES)],
            axis=0,
        )
        columns = jnp.dot(table[...], hot, preferred_element_type=F32).astype(BF16)
        picked[first] = columns[:, :LANES]
        picked[first + 1] = columns[:, LANES:]


def pack_kernel(features, heads, relations, tails, packed, rows, ids, sems):
    sources = (features, heads, relations, tails)
    targets = (rows, ids.at[0], ids.at[1], ids.at[2])
    copies = [
        pltpu.make_async_copy(source, target, sems.at[i])
        for i, (source, target) in enumerate(zip(sources, targets, strict=True))
    ]
    for copy in copies:
        copy.start()
    for copy in copies:
        copy.wait()
    width = features.shape[1]
    packed[:, :width] = rows[...]
    columns = [ids[0], ids[2], ids[1] // LANES, ids[1] % LANES]
    packed[:, width:] = jnp.concatenate(columns, axis=0).astype(F32).astype(BF16)


def early_kernel(rows, width, block, table, picked, ids):
    ids[...] = block[:, width:].astype(F32)
    me = lax.axis_index("grp").astype(jnp.int32)
    pick_relations(ids, range(block.shape[0] // rows), me, rows, table, picked)


def late_kernel(rows, width, skipped, block, table, begun, picked, ids):
    del begun
    ids[...] = block[:, width:].astype(F32)
    me = lax.axis_index("grp").astype(jnp.int32)
    pick_relations(ids, range(skipped, block.shape[0] // rows), me, rows, table, picked)


def sigmoid_parts(value):
    small = jnp.exp(-jnp.abs(value))
    softplus = jnp.maximum(value, 0.0) + jnp.log(1.0 + small)
    sigmoid = jnp.where(value >= 0.0, 1.0, small) / (1.0 + small)
    return softplus, sigmoid


def score_kernel(
    rows,
    keys,
    partner,
    mine,
    other,
    w_first,
    w_second,
    table,
    negatives,
    picked_mine,
    grad_out,
    loss_out,
    slope_out,
    hidden_out,
    encoded,
    ids,
    grads,
    picked_other,
    scores_kept,
    weights_kept,
    partner_kept,
    partner_sem,
):
    fetch = pltpu.make_async_copy(partner, partner_kept, partner_sem)
    fetch.start()
    width = w_first.shape[0]
    half = encoded.shape[1] // 2
    places = len(keys)
    all_rows = places * rows
    group_rows = 2 * rows
    members = (0, all_rows)
    me = lax.axis_index("grp").astype(jnp.int32)

    ids[:all_rows, :] = mine[:, width:].astype(F32)
    ids[all_rows:, :] = other[:, width:].astype(F32)
    features = jnp.concatenate([mine[:, :width], other[:, :width]], axis=0)
    pre_act = jnp.dot(features, w_first[...], preferred_element_type=F32)
    gate = 1.0 / (1.0 + jnp.exp(-pre_act))
    hidden = (pre_act * gate).astype(BF16)
    slope_out[...] = gate * (1.0 + pre_act * (1.0 - gate))
    hidden_out[...] = hidden
    encoded[...] = jnp.dot(hidden, w_second[...], preferred_element_type=F32).astype(BF16).astype(F32)
    pick_relations(ids.at[pl.ds(all_rows, all_rows)], range(places), me, rows, table, picked_other)

    labels = [(i ^ (me * rows)).astype(F32) for i in range(group_rows)]
    label_column = lax.broadcasted_iota(jnp.int32, (group_rows, 1), 0) ^ (me * rows)
    drawn = negatives[pl.ds(me, 1), :]
    counts = jnp.sum((drawn == label_column).astype(F32), axis=1, keepdims=True)
    negative_count = negatives.shape[1]
    label_column = label_column.astype(F32)
    fetch.wait()
    far_place = place_of(partner_kept[me, 0], keys)
    low_bit = far_place & -far_place

    def edge_ids(kind, place):
        return jnp.concatenate(
            [id_row(ids.at[pl.ds(base, all_rows)], kind, place, me, rows) for base in members], axis=1
        )

    def group_of(place):
        return jnp.concatenate(
            [encoded[pl.ds(pl.multiple_of(base + place * rows, rows), rows), :] for base in members],
            axis=0,
        )

    def relations_of(place):
        return jnp.concatenate([picked_mine[place], picked_other[place]], axis=1)

    for place in range(places):
        near_rows, far_rows = group_of(place), group_of(place ^ far_place)
        near_re, near_im = near_rows[:, :half], near_rows[:, half:]
        far_re, far_im = far_rows[:, :half], far_rows[:, half:]
        pairs = jnp.concatenate(
            [
                jnp.concatenate(
                    [
                        near_re[i : i + 1] * far_re + near_im[i : i + 1] * far_im,
                        near_re[i : i + 1] * far_im - near_im[i : i + 1] * far_re,
                    ],
                    axis=1,
                ).astype(BF16)
                for i in range(group_rows)
            ],
            axis=0,
        )
        scores = jnp.dot(pairs, relations_of(place), preferred_element_type=F32)
        head = edge_ids(HEAD, place)
        negative = jnp.zeros((group_rows, scores.shape[1]), F32)
        for i in range(group_rows):
            negative = jnp.where(
                head == labels[i], scores[i * group_rows : (i + 1) * group_rows], negative
            )
        scores_kept[place] = negative

    for place in range(places):
        negative = scores_kept[place]
        is_tail = edge_ids(TAIL, place) == label_column
        positive = jnp.sum(jnp.where(is_tail, negative, 0.0), axis=0, keepdims=True)
        loss, chance = sigmoid_parts(negative)
        loss_positive, chance_positive = sigmoid_parts(-positive)
        if place == 0:
            loss_out[...] = loss_positive + jnp.sum(loss * counts, axis=0, keepdims=True) / negative_count
        weight = (chance / negative_count).astype(BF16).astype(F32) * counts
        weights_kept[place] = (weight - jnp.where(is_tail, chance_positive, 0.0)).astype(BF16)

    for pair in range(places // 2):
        place = pair + (pair & -low_bit)
        far = place ^ far_place
        near_weight, far_weight = weights_kept[place], weights_kept[far]
        near_head, far_head = edge_ids(HEAD, place), edge_ids(HEAD, far)
        far_hot = (far_head == label_column).astype(BF16)
        near_rows, far_rows = group_of(place), group_of(far)
        near_re, near_im = near_rows[:, :half], near_rows[:, half:]
        far_re, far_im = far_rows[:, :half], far_rows[:, half:]
        weights = jnp.concatenate(
            [
                jnp.concatenate(
                    [near_weight * (near_head == labels[i]).astype(BF16), far_weight[i : i + 1] * far_hot],
                    axis=1,
                )
                for i in range(group_rows)
            ],
            axis=0,
        )
        relation = relations_of(place)
        relation = jnp.concatenate([relation[:half], -relation[half:]], axis=0)
        joint = lax.dot_general(
            weights,
            jnp.concatenate([relation, relations_of(far)], axis=1),
            (((1,), (1,)), ((), ())),
            preferred_element_type=F32,
        )
        far_grad_re = jnp.zeros((group_rows, half), F32)
        far_grad_im = jnp.zeros((group_rows, half), F32)
        near_grad = []
        for i in range(group_rows):
            part_re = joint[i * group_rows : (i + 1) * group_rows, :half]
            part_im = joint[i * group_rows : (i + 1) * group_rows, half:]
            row_re, row_im = near_re[i : i + 1], near_im[i : i + 1]
            far_grad_re = far_grad_re + (row_re * part_re + row_im * part_im)
            far_grad_im = far_grad_im + (row_im * part_re - row_re * part_im)
            near_grad.append(
                jnp.concatenate(
                    [
                        jnp.sum(far_re * part_re - far_im * part_im, axis=0, keepdims=True),
                        jnp.sum(far_im * part_re + far_re * part_im, axis=0, keepdims=True),
                    ],
                    axis=1,
                )
            )
        near_grad = jnp.concatenate(near_grad, axis=0)
        far_grad = jnp.concatenate([far_grad_re, far_grad_im], axis=1)
        for member, base in enumerate(members):
            span = slice(member * rows, (member + 1) * rows)
            grads[pl.ds(pl.multiple_of(base + place * rows, rows), rows), :] = near_grad[span]
            grads[pl.ds(pl.multiple_of(base + far * rows, rows), rows), :] = far_grad[span]
    grad_out[...] = grads[...].astype(BF16)


def total_kernel(
    limit,
    mine,
    other,
    grad_mine,
    grad_other,
    slope,
    hidden,
    w_second,
    loss_mine,
    loss_other,
    loss_out,
    first_out,
    second_out,
    first,
    second,
):
    me = lax.axis_index("grp").astype(jnp.int32)
    all_rows = mine.shape[0]
    width = first.shape[0]
    grad = jnp.concatenate(
        [
            grad_mine[:all_rows].astype(F32) + grad_other[all_rows:].astype(F32),
            grad_mine[all_rows:].astype(F32) + grad_other[:all_rows].astype(F32),
        ],
        axis=0,
    ).astype(BF16)
    across = (((0,), (0,)), ((), ()))
    total_second = lax.dot_general(hidden[...], grad, across, preferred_element_type=F32)
    grad_hidden = lax.dot_general(
        grad, w_second[...], (((1,), (1,)), ((), ())), preferred_element_type=F32
    )
    grad_pre = (grad_hidden * slope[...]).astype(BF16)
    features = jnp.concatenate([mine[:, :width], other[:, :width]], axis=0)
    total_first = lax.dot_general(features, grad_pre, across, preferred_element_type=F32)
    squares = jnp.sum(total_first * total_first, axis=(0, 1), keepdims=True) + jnp.sum(
        total_second * total_second, axis=(0, 1), keepdims=True
    )
    factor = jnp.minimum(1.0, limit / jnp.sqrt(squares + 1e-06))
    first[...] = total_first
    second[...] = total_second
    for source, target in ((first, first_out), (second, second_out)):
        share = target.shape[0]
        target[...] = source[pl.ds(pl.multiple_of(me * share, share), share), :] * factor
    edges = loss_out.shape[1]
    for member in range(2):
        loss_out[pl.ds(member, 1), :] = jnp.where(
            me == member, loss_mine[:, :edges], loss_other[:, edges:]
        )


def kernel_call(body, name, out_shape, scratch=(), flops=0, spaces=None, **more):
    vmem = pl.BlockSpec(memory_space=pltpu.VMEM)
    in_specs = None if spaces is None else [pl.BlockSpec(memory_space=space) for space in spaces]
    return pl.pallas_call(
        body,
        out_shape=out_shape,
        in_specs=in_specs,
        out_specs=jax.tree.map(lambda _: vmem, out_shape),
        scratch_shapes=scratch,
        compiler_params=pltpu.CompilerParams(vmem_limit_bytes=20 * 1024 * 1024),
        cost_estimate=pl.CostEstimate(flops=flops, bytes_accessed=0, transcendentals=0),
        name=name,
        **more,
    )


def together(
    features, w_first, w_second, relation_table, heads, relations, tails, negatives, partner
):
    rows, width = features.shape
    rounds, edges = heads.shape
    hidden_width, encoded_width = w_second.shape
    size = lax.axis_size("dom")
    keys = keys_of(size)
    steps = distances_of(size)
    all_rows = 2 * size * rows
    shape = jax.ShapeDtypeStruct
    table = jnp.pad(relation_table.T, ((0, 0), (0, -relation_table.shape[0] % LANES)))
    picked_shape = shape((size, encoded_width, edges), BF16)
    flops = 2 * table.size * edges

    block = kernel_call(
        pack_kernel,
        "pack",
        shape((rows, width + edges), BF16),
        [
            pltpu.VMEM(features.shape, BF16),
            pltpu.VMEM((3, rounds, edges), jnp.int32),
            pltpu.SemaphoreType.DMA((4,)),
        ],
        spaces=[pltpu.HBM] * 4,
    )(features, heads, relations, tails)
    for step in steps[:-1]:
        block, _ = join(block, "dom", step)
    early = block.shape[0] // rows
    picked = kernel_call(
        functools.partial(early_kernel, rows, width),
        "early",
        picked_shape,
        [pltpu.VMEM((early * rows, edges), F32)],
        flops * early,
        [pltpu.VMEM] * 2,
    )(block, table)
    mine, picked = join(block, "dom", steps[-1], picked)
    picked = kernel_call(
        functools.partial(late_kernel, rows, width, early),
        "late",
        picked_shape,
        [pltpu.VMEM((size * rows, edges), F32)],
        flops * (size - early),
        [pltpu.VMEM, pltpu.VMEM, pltpu.VMEM],
        input_output_aliases={2: 0},
    )(mine, table, picked)
    other = swap(mine, "grp", 1)

    grad, loss, slope, hidden = kernel_call(
        functools.partial(score_kernel, rows, keys),
        "scores",
        (
            shape((all_rows, encoded_width), BF16),
            shape((1, 2 * edges), F32),
            shape((all_rows, hidden_width), F32),
            shape((all_rows, hidden_width), BF16),
        ),
        [
            pltpu.VMEM((all_rows, encoded_width), F32),
            pltpu.VMEM((all_rows, edges), F32),
            pltpu.VMEM((all_rows, encoded_width), F32),
            pltpu.VMEM(picked_shape.shape, BF16),
            pltpu.VMEM((size, 2 * rows, 2 * edges), F32),
            pltpu.VMEM((size, 2 * rows, 2 * edges), BF16),
            pltpu.SMEM(partner.shape, jnp.int32),
            pltpu.SemaphoreType.DMA,
        ],
        flops * size * 2,
        [pl.ANY] + [pltpu.VMEM] * 7,
    )(partner, mine, other, w_first, w_second, table, negatives, picked)
    grad_other = swap(grad, "grp", 1)
    loss_other = swap(loss, "grp", 1)
    return kernel_call(
        functools.partial(total_kernel, math.sqrt(w_first.size + w_second.size)),
        "totals",
        (
            shape((rounds, edges), F32),
            shape((w_first.shape[0] // 2, w_first.shape[1]), F32),
            shape((w_second.shape[0] // 2, w_second.shape[1]), F32),
        ),
        [pltpu.VMEM(w_first.shape, F32), pltpu.VMEM(w_second.shape, F32)],
        0,
        [pltpu.VMEM] * 9,
    )(mine, other, grad, grad_other, slope, hidden, w_second, loss, loss_other)


def solution(mesh):
    def per_device(features, w_first, w_second, relation_table, heads, relations, tails, *rest):
        rounds, edges = heads.shape
        rows = features.shape[0]
        fits = (
            mesh.shape["grp"] == rounds == ROUNDS == 2
            and edges == LANES
            and 4 * rounds == rows
            and mesh.shape["dom"] >= 8
        )
        plan = together if fits else spread
        return plan(features, w_first, w_second, relation_table, heads, relations, tails, *rest)

    return jax.shard_map(
        per_device,
        mesh=mesh,
        in_specs=(
            P(("dom", "grp"), None),
            P(),
            P(),
            P(),
            P(None, ("dom", "grp")),
            P(None, ("dom", "grp")),
            P(None, ("dom", "grp")),
            P(),
            P(),
        ),
        out_specs=(P(None, ("dom", "grp")), P("grp", None), P("grp", None)),
        check_vma=False,
    )
```

```python
import functools
import math

import jax
import jax.numpy as jnp
from jax import lax
from jax.experimental import pallas as pl
from jax.experimental.pallas import tpu as pltpu
from jax.sharding import PartitionSpec as P

LANES = 128
F32 = jnp.float32
BF16 = jnp.bfloat16


def partner_2(value, axis, distance):
    return lax.ppermute(value, axis, [(i, i ^ 1 << distance) for i in range(lax.axis_size(axis))])


def encode(rows, w_first, w_second):
    pre_act = jnp.dot(rows, w_first, preferred_element_type=jnp.float32)
    hidden = jax.nn.silu(pre_act).astype(jnp.bfloat16)
    encoded = jnp.dot(hidden, w_second, preferred_element_type=jnp.float32).astype(jnp.bfloat16)
    return (pre_act, hidden, encoded)


def backward(rows, pre_act, hidden, grad_rows, w_second):
    term_second = lax.dot_general(
        hidden, grad_rows, (((0,), (0,)), ((), ())), preferred_element_type=jnp.float32
    )
    grad_hidden = lax.dot_general(
        grad_rows, w_second, (((1,), (1,)), ((), ())), preferred_element_type=jnp.float32
    )
    sigmoid_pre = jax.nn.sigmoid(pre_act)
    silu_slope = sigmoid_pre * (1.0 + pre_act * (1.0 - sigmoid_pre))
    grad_pre = (grad_hidden * silu_slope).astype(jnp.bfloat16)
    term_first = lax.dot_general(
        rows, grad_pre, (((0,), (0,)), ((), ())), preferred_element_type=jnp.float32
    )
    return (term_first, term_second)


def row_select(ids, row_count):
    return ids[:, None] == jnp.arange(row_count, dtype=jnp.int32)[None, :]


def pick_rows(selector, table):
    return jnp.dot(selector.astype(jnp.bfloat16), table, preferred_element_type=jnp.float32)


def add_into_rows(selector, values):
    return lax.dot_general(
        selector.astype(jnp.float32),
        values,
        (((0,), (0,)), ((), ())),
        precision=lax.Precision.HIGHEST,
        preferred_element_type=jnp.float32,
    )


def score_block(own, other, relation_table, head_ids, relation_ids, tail_ids, negative_ids):
    half_width = own.shape[1] // 2
    row_count = own.shape[0]
    head_select = row_select(head_ids, row_count)
    tail_select = row_select(tail_ids, row_count)
    negative_select = row_select(negative_ids, row_count)
    head_rows = pick_rows(head_select, own)
    rel_rows = jnp.take(relation_table, relation_ids, axis=0).astype(jnp.float32)
    tail_rows = pick_rows(tail_select, other)
    negative_rows = pick_rows(negative_select, other).astype(jnp.bfloat16)
    head_real, head_imag = (head_rows[:, :half_width], head_rows[:, half_width:])
    rel_real, rel_imag = (rel_rows[:, :half_width], rel_rows[:, half_width:])
    query = jnp.concatenate(
        [head_real * rel_real - head_imag * rel_imag, head_real * rel_imag + head_imag * rel_real],
        axis=1,
    ).astype(jnp.bfloat16)
    query_wide = query.astype(jnp.float32)
    positive = jnp.sum(query_wide * tail_rows, axis=1)
    negative = lax.dot_general(
        query, negative_rows, (((1,), (1,)), ((), ())), preferred_element_type=jnp.float32
    )
    edge_loss = (
        jax.nn.softplus(-positive) + jnp.sum(jax.nn.softplus(negative), axis=1) / negative.shape[1]
    )
    weight_neg = (jax.nn.sigmoid(negative) / negative.shape[1]).astype(jnp.bfloat16)
    weight_pos = -jax.nn.sigmoid(-positive)
    grad_query = weight_pos[:, None] * tail_rows + jnp.dot(
        weight_neg, negative_rows, preferred_element_type=jnp.float32
    )
    grad_tail = weight_pos[:, None] * query_wide
    grad_negative = lax.dot_general(
        weight_neg, query, (((0,), (0,)), ((), ())), preferred_element_type=jnp.float32
    )
    grad_real, grad_imag = (grad_query[:, :half_width], grad_query[:, half_width:])
    grad_head = jnp.concatenate(
        [grad_real * rel_real + grad_imag * rel_imag, grad_imag * rel_real - grad_real * rel_imag],
        axis=1,
    )
    own_part = add_into_rows(head_select, grad_head)
    far_part = add_into_rows(tail_select, grad_tail) + add_into_rows(negative_select, grad_negative)
    return (edge_loss, own_part, far_part)


def route_rows(payload, xor_mask, bit_count, mover):
    for bit_level in range(bit_count):
        swapped = mover(payload, bit_level)
        payload = jnp.where(xor_mask >> bit_level & 1 == 1, swapped, payload)
    return payload


def spread(
    features, w_first, w_second, relation_table, heads, relations, tails, negatives, partner
):
    pre_act, hidden, encoded = encode(features, w_first, w_second)
    own_block = lax.all_gather(encoded, "grp", axis=0, tiled=True)
    bit_count = lax.axis_size("dom").bit_length() - 1
    total_first = jnp.zeros(w_first.shape, jnp.float32)
    total_second = jnp.zeros(w_second.shape, jnp.float32)
    own_acc = jnp.zeros(own_block.shape, jnp.float32)
    losses = []
    for bucket in range(heads.shape[0]):
        xor_mask = partner[bucket, 0]
        arrived = route_rows(
            encoded,
            xor_mask,
            bit_count,
            lambda payload, bit_level: partner_2(payload, "dom", bit_level),
        )
        far_block = lax.all_gather(arrived, "grp", axis=0, tiled=True)
        edge_loss, own_part, far_part = score_block(
            own_block,
            far_block,
            relation_table,
            heads[bucket],
            relations[bucket],
            tails[bucket],
            negatives[bucket],
        )
        losses.append(edge_loss)
        own_acc = own_acc + own_part
        far_grad = lax.psum_scatter(
            far_part.astype(jnp.bfloat16), "grp", scatter_dimension=0, tiled=True
        )
        returned = route_rows(
            far_grad,
            xor_mask,
            bit_count,
            lambda payload, bit_level: partner_2(payload, "dom", bit_level),
        )
        term_first, term_second = backward(features, pre_act, hidden, returned, w_second)
        total_first = total_first + term_first
        total_second = total_second + term_second
    own_grad = lax.psum_scatter(
        own_acc.astype(jnp.bfloat16), "grp", scatter_dimension=0, tiled=True
    )
    term_first, term_second = backward(features, pre_act, hidden, own_grad, w_second)
    total_first = total_first + term_first
    total_second = total_second + term_second
    part_first, part_second = (
        lax.psum_scatter(
            total_first.astype(jnp.bfloat16), "grp", scatter_dimension=0, tiled=True
        ).astype(jnp.float32),
        lax.psum_scatter(
            total_second.astype(jnp.bfloat16), "grp", scatter_dimension=0, tiled=True
        ).astype(jnp.float32),
    )
    summed_first, summed_second = lax.psum((part_first, part_second), "dom")
    local_squares = jnp.sum(summed_first * summed_first) + jnp.sum(summed_second * summed_second)
    squares = lax.psum(local_squares, "grp")
    factor = jnp.minimum(1.0, math.sqrt(w_first.size + w_second.size) / jnp.sqrt(squares + 1e-06))
    return (jnp.stack(losses), summed_first * factor, summed_second * factor)


ROUNDS = 2
HEAD, TAIL, HIGH, LOW = 0, 1, 2, 3


def swap(value, axis, distance):
    return lax.ppermute(value, axis, [(i, i ^ distance) for i in range(lax.axis_size(axis))])


def distances_of(size):
    steps = []
    while size > 1:
        radix = min(size, 4)
        size //= radix
        steps.append([i * size for i in range(radix - 1, 0, -1)])
    return steps


def join(value, axis, step, beside):
    arrived = [swap(value, axis, distance) for distance in step]
    *arrived, beside = lax.optimization_barrier((*arrived[::-1], beside))
    return jnp.concatenate([value] + arrived[::-1], axis=0), beside


def keys_of(size):
    keys = [0]
    for step in distances_of(size):
        keys = keys + [key ^ distance for distance in step for key in keys]
    return keys


def place_of(mask, keys):
    place, bit = jnp.int32(0), 1
    while bit < len(keys):
        place = place ^ jnp.where((mask & bit) != 0, keys.index(bit), 0)
        bit *= 2
    return place


def id_row(ids, kind, place, me, rows):
    return ids[pl.ds(place * rows + kind * ROUNDS + me, 1), :]


def pick_relations(low, high, table):
    low_column = lax.broadcasted_iota(jnp.int32, (LANES, 1), 0).astype(F32)
    low_hot = (low == low_column).astype(BF16)
    hot = jnp.concatenate(
        [low_hot * (high == float(block)).astype(BF16) for block in range(table.shape[1] // LANES)],
        axis=0,
    )
    columns = jnp.dot(table[...], hot, preferred_element_type=F32).astype(BF16)
    return columns[:, :LANES], columns[:, LANES:]


def pick_blocks(ids, places, me, rows, table, picked):
    for first in range(places.start, places.stop, 2):
        low, high = [
            jnp.concatenate([id_row(ids, kind, place, me, rows) for place in (first, first + 1)], axis=1)
            for kind in (LOW, HIGH)
        ]
        picked[first], picked[first + 1] = pick_relations(low, high, table)


def pack_kernel(features, heads, relations, tails, packed, rows, ids, sems):
    sources = (features, heads, relations, tails)
    targets = (rows, ids.at[0], ids.at[1], ids.at[2])
    copies = [
        pltpu.make_async_copy(source, target, sems.at[i])
        for i, (source, target) in enumerate(zip(sources, targets, strict=True))
    ]
    for copy in copies:
        copy.start()
    for copy in copies:
        copy.wait()
    width = features.shape[1]
    packed[:, :width] = rows[...]
    columns = [ids[0], ids[2], ids[1] // LANES, ids[1] % LANES]
    packed[:, width:] = jnp.concatenate(columns, axis=0).astype(F32).astype(BF16)


def early_kernel(rows, width, block, other_ids, table, picked, picked_other, ids, ids_other):
    ids[...] = block[:, width:].astype(F32)
    ids_other[...] = other_ids[...].astype(F32)
    me = lax.axis_index("grp").astype(jnp.int32)
    for place in range(block.shape[0] // rows):
        low, high = [
            jnp.concatenate([id_row(member, kind, place, me, rows) for member in (ids, ids_other)], axis=1)
            for kind in (LOW, HIGH)
        ]
        picked[place], picked_other[place] = pick_relations(low, high, table)


def late_kernel(rows, width, skipped, block, table, begun, picked, ids):
    del begun
    ids[...] = block[:, width:].astype(F32)
    me = lax.axis_index("grp").astype(jnp.int32)
    pick_blocks(ids, range(skipped, block.shape[0] // rows), me, rows, table, picked)


def sigmoid_parts(value):
    small = jnp.exp(-jnp.abs(value))
    softplus = jnp.maximum(value, 0.0) + jnp.log(1.0 + small)
    sigmoid = jnp.where(value >= 0.0, 1.0, small) / (1.0 + small)
    return softplus, sigmoid


def score_kernel(
    rows,
    keys,
    partner,
    mine,
    other,
    w_first,
    w_second,
    table,
    negatives,
    picked_mine,
    picked_early,
    grad_out,
    loss_out,
    slope_out,
    hidden_out,
    encoded,
    ids,
    grads,
    picked_other,
    scores_kept,
    weights_kept,
    partner_kept,
    partner_sem,
):
    fetch = pltpu.make_async_copy(partner, partner_kept, partner_sem)
    fetch.start()
    width = w_first.shape[0]
    half = encoded.shape[1] // 2
    places = len(keys)
    all_rows = places * rows
    group_rows = 2 * rows
    members = (0, all_rows)
    me = lax.axis_index("grp").astype(jnp.int32)

    ids[:all_rows, :] = mine[:, width:].astype(F32)
    ids[all_rows:, :] = other[:, width:].astype(F32)
    features = jnp.concatenate([mine[:, :width], other[:, :width]], axis=0)
    pre_act = jnp.dot(features, w_first[...], preferred_element_type=F32)
    gate = 1.0 / (1.0 + jnp.exp(-pre_act))
    hidden = (pre_act * gate).astype(BF16)
    slope_out[...] = gate * (1.0 + pre_act * (1.0 - gate))
    hidden_out[...] = hidden
    encoded[...] = jnp.dot(hidden, w_second[...], preferred_element_type=F32).astype(BF16).astype(F32)
    early = picked_early.shape[0]
    picked_other[:early] = picked_early[...]
    pick_blocks(ids.at[pl.ds(all_rows, all_rows)], range(early, places), me, rows, table, picked_other)

    labels = [(i ^ (me * rows)).astype(F32) for i in range(group_rows)]
    label_column = lax.broadcasted_iota(jnp.int32, (group_rows, 1), 0) ^ (me * rows)
    drawn = negatives[pl.ds(me, 1), :]
    counts = jnp.sum((drawn == label_column).astype(F32), axis=1, keepdims=True)
    negative_count = negatives.shape[1]
    label_column = label_column.astype(F32)
    fetch.wait()
    far_place = place_of(partner_kept[me, 0], keys)
    low_bit = far_place & -far_place

    def edge_ids(kind, place):
        return jnp.concatenate(
            [id_row(ids.at[pl.ds(base, all_rows)], kind, place, me, rows) for base in members], axis=1
        )

    def group_of(place):
        return jnp.concatenate(
            [encoded[pl.ds(pl.multiple_of(base + place * rows, rows), rows), :] for base in members],
            axis=0,
        )

    def relations_of(place):
        return jnp.concatenate([picked_mine[place], picked_other[place]], axis=1)

    for place in range(places):
        near_rows, far_rows = group_of(place), group_of(place ^ far_place)
        near_re, near_im = near_rows[:, :half], near_rows[:, half:]
        far_re, far_im = far_rows[:, :half], far_rows[:, half:]
        pairs = jnp.concatenate(
            [
                jnp.concatenate(
                    [
                        near_re[i : i + 1] * far_re + near_im[i : i + 1] * far_im,
                        near_re[i : i + 1] * far_im - near_im[i : i + 1] * far_re,
                    ],
                    axis=1,
                ).astype(BF16)
                for i in range(group_rows)
            ],
            axis=0,
        )
        scores = jnp.dot(pairs, relations_of(place), preferred_element_type=F32)
        head = edge_ids(HEAD, place)
        negative = jnp.zeros((group_rows, scores.shape[1]), F32)
        for i in range(group_rows):
            negative = jnp.where(
                head == labels[i], scores[i * group_rows : (i + 1) * group_rows], negative
            )
        scores_kept[place] = negative

    for place in range(places):
        negative = scores_kept[place]
        is_tail = edge_ids(TAIL, place) == label_column
        positive = jnp.sum(jnp.where(is_tail, negative, 0.0), axis=0, keepdims=True)
        loss, chance = sigmoid_parts(negative)
        loss_positive, chance_positive = sigmoid_parts(-positive)
        if place == 0:
            loss_out[...] = loss_positive + jnp.sum(loss * counts, axis=0, keepdims=True) / negative_count
        weight = (chance / negative_count).astype(BF16).astype(F32) * counts
        weights_kept[place] = (weight - jnp.where(is_tail, chance_positive, 0.0)).astype(BF16)

    for pair in range(places // 2):
        place = pair + (pair & -low_bit)
        far = place ^ far_place
        near_weight, far_weight = weights_kept[place], weights_kept[far]
        near_head, far_head = edge_ids(HEAD, place), edge_ids(HEAD, far)
        far_hot = (far_head == label_column).astype(BF16)
        near_rows, far_rows = group_of(place), group_of(far)
        near_re, near_im = near_rows[:, :half], near_rows[:, half:]
        far_re, far_im = far_rows[:, :half], far_rows[:, half:]
        weights = jnp.concatenate(
            [
                jnp.concatenate(
                    [near_weight * (near_head == labels[i]).astype(BF16), far_weight[i : i + 1] * far_hot],
                    axis=1,
                )
                for i in range(group_rows)
            ],
            axis=0,
        )
        relation = relations_of(place)
        relation = jnp.concatenate([relation[:half], -relation[half:]], axis=0)
        joint = lax.dot_general(
            weights,
            jnp.concatenate([relation, relations_of(far)], axis=1),
            (((1,), (1,)), ((), ())),
            preferred_element_type=F32,
        )
        far_grad_re = jnp.zeros((group_rows, half), F32)
        far_grad_im = jnp.zeros((group_rows, half), F32)
        near_grad = []
        for i in range(group_rows):
            part_re = joint[i * group_rows : (i + 1) * group_rows, :half]
            part_im = joint[i * group_rows : (i + 1) * group_rows, half:]
            row_re, row_im = near_re[i : i + 1], near_im[i : i + 1]
            far_grad_re = far_grad_re + (row_re * part_re + row_im * part_im)
            far_grad_im = far_grad_im + (row_im * part_re - row_re * part_im)
            near_grad.append(
                jnp.concatenate(
                    [
                        jnp.sum(far_re * part_re - far_im * part_im, axis=0, keepdims=True),
                        jnp.sum(far_im * part_re + far_re * part_im, axis=0, keepdims=True),
                    ],
                    axis=1,
                )
            )
        near_grad = jnp.concatenate(near_grad, axis=0)
        far_grad = jnp.concatenate([far_grad_re, far_grad_im], axis=1)
        for member, base in enumerate(members):
            span = slice(member * rows, (member + 1) * rows)
            grads[pl.ds(pl.multiple_of(base + place * rows, rows), rows), :] = near_grad[span]
            grads[pl.ds(pl.multiple_of(base + far * rows, rows), rows), :] = far_grad[span]
    grad_out[...] = grads[...].astype(BF16)


def total_kernel(
    limit,
    mine,
    other,
    grad_mine,
    grad_other,
    slope,
    hidden,
    w_second,
    loss_mine,
    loss_other,
    loss_out,
    first_out,
    second_out,
    first,
    second,
):
    me = lax.axis_index("grp").astype(jnp.int32)
    all_rows = mine.shape[0]
    width = first.shape[0]
    grad = jnp.concatenate(
        [
            grad_mine[:all_rows].astype(F32) + grad_other[all_rows:].astype(F32),
            grad_mine[all_rows:].astype(F32) + grad_other[:all_rows].astype(F32),
        ],
        axis=0,
    ).astype(BF16)
    across = (((0,), (0,)), ((), ()))
    total_second = lax.dot_general(hidden[...], grad, across, preferred_element_type=F32)
    grad_hidden = lax.dot_general(
        grad, w_second[...], (((1,), (1,)), ((), ())), preferred_element_type=F32
    )
    grad_pre = (grad_hidden * slope[...]).astype(BF16)
    features = jnp.concatenate([mine[:, :width], other[:, :width]], axis=0)
    total_first = lax.dot_general(features, grad_pre, across, preferred_element_type=F32)
    squares = jnp.sum(total_first * total_first, axis=(0, 1), keepdims=True) + jnp.sum(
        total_second * total_second, axis=(0, 1), keepdims=True
    )
    factor = jnp.minimum(1.0, limit / jnp.sqrt(squares + 1e-06))
    first[...] = total_first
    second[...] = total_second
    for source, target in ((first, first_out), (second, second_out)):
        share = target.shape[0]
        target[...] = source[pl.ds(pl.multiple_of(me * share, share), share), :] * factor
    edges = loss_out.shape[1]
    for member in range(2):
        loss_out[pl.ds(member, 1), :] = jnp.where(
            me == member, loss_mine[:, :edges], loss_other[:, edges:]
        )


def kernel_call(body, name, out_shape, scratch=(), flops=0, spaces=None, mebibytes=20, **more):
    vmem = pl.BlockSpec(memory_space=pltpu.VMEM)
    in_specs = None if spaces is None else [pl.BlockSpec(memory_space=space) for space in spaces]
    return pl.pallas_call(
        body,
        out_shape=out_shape,
        in_specs=in_specs,
        out_specs=jax.tree.map(lambda _: vmem, out_shape),
        scratch_shapes=scratch,
        compiler_params=pltpu.CompilerParams(vmem_limit_bytes=mebibytes * 1024 * 1024),
        cost_estimate=pl.CostEstimate(flops=flops, bytes_accessed=0, transcendentals=0),
        name=name,
        **more,
    )


def together(
    features, w_first, w_second, relation_table, heads, relations, tails, negatives, partner
):
    rows, width = features.shape
    rounds, edges = heads.shape
    hidden_width, encoded_width = w_second.shape
    size = lax.axis_size("dom")
    keys = keys_of(size)
    steps = distances_of(size)
    all_rows = 2 * size * rows
    shape = jax.ShapeDtypeStruct
    table = jnp.pad(relation_table.T, ((0, 0), (0, -relation_table.shape[0] % LANES)))
    picked_shape = shape((size, encoded_width, edges), BF16)
    flops = 2 * table.size * edges

    block = kernel_call(
        pack_kernel,
        "pack",
        shape((rows, width + edges), BF16),
        [
            pltpu.VMEM(features.shape, BF16),
            pltpu.VMEM((3, rounds, edges), jnp.int32),
            pltpu.SemaphoreType.DMA((4,)),
        ],
        spaces=[pltpu.HBM] * 4,
        mebibytes=60,
    )(features, heads, relations, tails)
    for step in steps[:-1]:
        block, table = join(block, "dom", step, table)
    early = block.shape[0] // rows
    early_ids = swap(block[:, width:], "grp", 1)
    picked, picked_early = kernel_call(
        functools.partial(early_kernel, rows, width),
        "early",
        (picked_shape, shape((early, encoded_width, edges), BF16)),
        [pltpu.VMEM((early * rows, edges), F32)] * 2,
        flops * early * 2,
        [pltpu.VMEM] * 3,
    )(block, early_ids, table)
    mine, picked = join(block, "dom", steps[-1], picked)
    picked = kernel_call(
        functools.partial(late_kernel, rows, width, early),
        "late",
        picked_shape,
        [pltpu.VMEM((size * rows, edges), F32)],
        flops * (size - early),
        [pltpu.VMEM, pltpu.VMEM, pltpu.VMEM],
        input_output_aliases={2: 0},
    )(mine, table, picked)
    other = swap(mine, "grp", 1)

    grad, loss, slope, hidden = kernel_call(
        functools.partial(score_kernel, rows, keys),
        "scores",
        (
            shape((all_rows, encoded_width), BF16),
            shape((1, 2 * edges), F32),
            shape((all_rows, hidden_width), F32),
            shape((all_rows, hidden_width), BF16),
        ),
        [
            pltpu.VMEM((all_rows, encoded_width), F32),
            pltpu.VMEM((all_rows, edges), F32),
            pltpu.VMEM((all_rows, encoded_width), F32),
            pltpu.VMEM(picked_shape.shape, BF16),
            pltpu.VMEM((size, 2 * rows, 2 * edges), F32),
            pltpu.VMEM((size, 2 * rows, 2 * edges), BF16),
            pltpu.SMEM(partner.shape, jnp.int32),
            pltpu.SemaphoreType.DMA,
        ],
        flops * size * 2,
        [pl.ANY] + [pltpu.VMEM] * 8,
    )(partner, mine, other, w_first, w_second, table, negatives, picked, picked_early)
    grad_other = swap(grad, "grp", 1)
    loss_other = swap(loss, "grp", 1)
    return kernel_call(
        functools.partial(total_kernel, math.sqrt(w_first.size + w_second.size)),
        "totals",
        (
            shape((rounds, edges), F32),
            shape((w_first.shape[0] // 2, w_first.shape[1]), F32),
            shape((w_second.shape[0] // 2, w_second.shape[1]), F32),
        ),
        [pltpu.VMEM(w_first.shape, F32), pltpu.VMEM(w_second.shape, F32)],
        0,
        [pltpu.VMEM] * 9,
    )(mine, other, grad, grad_other, slope, hidden, w_second, loss, loss_other)


def solution(mesh):
    def per_device(features, w_first, w_second, relation_table, heads, relations, tails, *rest):
        rounds, edges = heads.shape
        rows = features.shape[0]
        fits = (
            mesh.shape["grp"] == rounds == ROUNDS == 2
            and edges == LANES
            and 4 * rounds == rows
            and mesh.shape["dom"] >= 8
        )
        plan = together if fits else spread
        return plan(features, w_first, w_second, relation_table, heads, relations, tails, *rest)

    return jax.shard_map(
        per_device,
        mesh=mesh,
        in_specs=(
            P(("dom", "grp"), None),
            P(),
            P(),
            P(),
            P(None, ("dom", "grp")),
            P(None, ("dom", "grp")),
            P(None, ("dom", "grp")),
            P(),
            P(),
        ),
        out_specs=(P(None, ("dom", "grp")), P("grp", None), P("grp", None)),
        check_vma=False,
    )
```

```python
import functools
import math

import jax
import jax.numpy as jnp
from jax import lax
from jax.experimental import pallas as pl
from jax.experimental.pallas import tpu as pltpu
from jax.sharding import PartitionSpec as P

LANES = 128
F32 = jnp.float32
BF16 = jnp.bfloat16


def partner_2(value, axis, distance):
    return lax.ppermute(value, axis, [(i, i ^ 1 << distance) for i in range(lax.axis_size(axis))])


def encode(rows, w_first, w_second):
    pre_act = jnp.dot(rows, w_first, preferred_element_type=jnp.float32)
    hidden = jax.nn.silu(pre_act).astype(jnp.bfloat16)
    encoded = jnp.dot(hidden, w_second, preferred_element_type=jnp.float32).astype(jnp.bfloat16)
    return (pre_act, hidden, encoded)


def backward(rows, pre_act, hidden, grad_rows, w_second):
    term_second = lax.dot_general(
        hidden, grad_rows, (((0,), (0,)), ((), ())), preferred_element_type=jnp.float32
    )
    grad_hidden = lax.dot_general(
        grad_rows, w_second, (((1,), (1,)), ((), ())), preferred_element_type=jnp.float32
    )
    sigmoid_pre = jax.nn.sigmoid(pre_act)
    silu_slope = sigmoid_pre * (1.0 + pre_act * (1.0 - sigmoid_pre))
    grad_pre = (grad_hidden * silu_slope).astype(jnp.bfloat16)
    term_first = lax.dot_general(
        rows, grad_pre, (((0,), (0,)), ((), ())), preferred_element_type=jnp.float32
    )
    return (term_first, term_second)


def row_select(ids, row_count):
    return ids[:, None] == jnp.arange(row_count, dtype=jnp.int32)[None, :]


def pick_rows(selector, table):
    return jnp.dot(selector.astype(jnp.bfloat16), table, preferred_element_type=jnp.float32)


def add_into_rows(selector, values):
    return lax.dot_general(
        selector.astype(jnp.float32),
        values,
        (((0,), (0,)), ((), ())),
        precision=lax.Precision.HIGHEST,
        preferred_element_type=jnp.float32,
    )


def score_block(own, other, relation_table, head_ids, relation_ids, tail_ids, negative_ids):
    half_width = own.shape[1] // 2
    row_count = own.shape[0]
    head_select = row_select(head_ids, row_count)
    tail_select = row_select(tail_ids, row_count)
    negative_select = row_select(negative_ids, row_count)
    head_rows = pick_rows(head_select, own)
    rel_rows = jnp.take(relation_table, relation_ids, axis=0).astype(jnp.float32)
    tail_rows = pick_rows(tail_select, other)
    negative_rows = pick_rows(negative_select, other).astype(jnp.bfloat16)
    head_real, head_imag = (head_rows[:, :half_width], head_rows[:, half_width:])
    rel_real, rel_imag = (rel_rows[:, :half_width], rel_rows[:, half_width:])
    query = jnp.concatenate(
        [head_real * rel_real - head_imag * rel_imag, head_real * rel_imag + head_imag * rel_real],
        axis=1,
    ).astype(jnp.bfloat16)
    query_wide = query.astype(jnp.float32)
    positive = jnp.sum(query_wide * tail_rows, axis=1)
    negative = lax.dot_general(
        query, negative_rows, (((1,), (1,)), ((), ())), preferred_element_type=jnp.float32
    )
    edge_loss = (
        jax.nn.softplus(-positive) + jnp.sum(jax.nn.softplus(negative), axis=1) / negative.shape[1]
    )
    weight_neg = (jax.nn.sigmoid(negative) / negative.shape[1]).astype(jnp.bfloat16)
    weight_pos = -jax.nn.sigmoid(-positive)
    grad_query = weight_pos[:, None] * tail_rows + jnp.dot(
        weight_neg, negative_rows, preferred_element_type=jnp.float32
    )
    grad_tail = weight_pos[:, None] * query_wide
    grad_negative = lax.dot_general(
        weight_neg, query, (((0,), (0,)), ((), ())), preferred_element_type=jnp.float32
    )
    grad_real, grad_imag = (grad_query[:, :half_width], grad_query[:, half_width:])
    grad_head = jnp.concatenate(
        [grad_real * rel_real + grad_imag * rel_imag, grad_imag * rel_real - grad_real * rel_imag],
        axis=1,
    )
    own_part = add_into_rows(head_select, grad_head)
    far_part = add_into_rows(tail_select, grad_tail) + add_into_rows(negative_select, grad_negative)
    return (edge_loss, own_part, far_part)


def route_rows(payload, xor_mask, bit_count, mover):
    for bit_level in range(bit_count):
        swapped = mover(payload, bit_level)
        payload = jnp.where(xor_mask >> bit_level & 1 == 1, swapped, payload)
    return payload


def spread(
    features, w_first, w_second, relation_table, heads, relations, tails, negatives, partner
):
    pre_act, hidden, encoded = encode(features, w_first, w_second)
    own_block = lax.all_gather(encoded, "grp", axis=0, tiled=True)
    bit_count = lax.axis_size("dom").bit_length() - 1
    total_first = jnp.zeros(w_first.shape, jnp.float32)
    total_second = jnp.zeros(w_second.shape, jnp.float32)
    own_acc = jnp.zeros(own_block.shape, jnp.float32)
    losses = []
    for bucket in range(heads.shape[0]):
        xor_mask = partner[bucket, 0]
        arrived = route_rows(
            encoded,
            xor_mask,
            bit_count,
            lambda payload, bit_level: partner_2(payload, "dom", bit_level),
        )
        far_block = lax.all_gather(arrived, "grp", axis=0, tiled=True)
        edge_loss, own_part, far_part = score_block(
            own_block,
            far_block,
            relation_table,
            heads[bucket],
            relations[bucket],
            tails[bucket],
            negatives[bucket],
        )
        losses.append(edge_loss)
        own_acc = own_acc + own_part
        far_grad = lax.psum_scatter(
            far_part.astype(jnp.bfloat16), "grp", scatter_dimension=0, tiled=True
        )
        returned = route_rows(
            far_grad,
            xor_mask,
            bit_count,
            lambda payload, bit_level: partner_2(payload, "dom", bit_level),
        )
        term_first, term_second = backward(features, pre_act, hidden, returned, w_second)
        total_first = total_first + term_first
        total_second = total_second + term_second
    own_grad = lax.psum_scatter(
        own_acc.astype(jnp.bfloat16), "grp", scatter_dimension=0, tiled=True
    )
    term_first, term_second = backward(features, pre_act, hidden, own_grad, w_second)
    total_first = total_first + term_first
    total_second = total_second + term_second
    part_first, part_second = (
        lax.psum_scatter(
            total_first.astype(jnp.bfloat16), "grp", scatter_dimension=0, tiled=True
        ).astype(jnp.float32),
        lax.psum_scatter(
            total_second.astype(jnp.bfloat16), "grp", scatter_dimension=0, tiled=True
        ).astype(jnp.float32),
    )
    summed_first, summed_second = lax.psum((part_first, part_second), "dom")
    local_squares = jnp.sum(summed_first * summed_first) + jnp.sum(summed_second * summed_second)
    squares = lax.psum(local_squares, "grp")
    factor = jnp.minimum(1.0, math.sqrt(w_first.size + w_second.size) / jnp.sqrt(squares + 1e-06))
    return (jnp.stack(losses), summed_first * factor, summed_second * factor)


ROUNDS = 2
HEAD, TAIL, HIGH, LOW = 0, 1, 2, 3


def swap(value, axis, distance):
    return lax.ppermute(value, axis, [(i, i ^ distance) for i in range(lax.axis_size(axis))])


def distances_of(size):
    steps = []
    while size > 1:
        radix = min(size, 4)
        size //= radix
        steps.append([i * size for i in range(radix - 1, 0, -1)])
    return steps


def arrivals(value, axis, step):
    return [swap(value, axis, distance) for distance in step]


def join(value, arrived, *beside):
    count = len(arrived)
    done = lax.optimization_barrier((*arrived, *beside))
    return jnp.concatenate([value, *done[:count]], axis=0), *done[count:]


def keys_of(size):
    keys = [0]
    for step in distances_of(size):
        keys = keys + [key ^ distance for distance in step for key in keys]
    return keys


def place_of(mask, keys):
    place, bit = jnp.int32(0), 1
    while bit < len(keys):
        place = place ^ jnp.where((mask & bit) != 0, keys.index(bit), 0)
        bit *= 2
    return place


def id_row(ids, kind, place, me, rows):
    return ids[pl.ds(place * rows + kind * ROUNDS + me, 1), :]


def pick_relations(low, high, table):
    low_column = lax.broadcasted_iota(jnp.int32, (LANES, 1), 0).astype(F32)
    low_hot = (low == low_column).astype(BF16)
    hot = jnp.concatenate(
        [low_hot * (high == float(block)).astype(BF16) for block in range(table.shape[1] // LANES)],
        axis=0,
    )
    columns = jnp.dot(table[...], hot, preferred_element_type=F32).astype(BF16)
    return columns[:, :LANES], columns[:, LANES:]


def pick_blocks(ids, places, me, rows, table, picked):
    for first in range(places.start, places.stop, 2):
        low, high = [
            jnp.concatenate([id_row(ids, kind, place, me, rows) for place in (first, first + 1)], axis=1)
            for kind in (LOW, HIGH)
        ]
        picked[first], picked[first + 1] = pick_relations(low, high, table)


def pack_kernel(features, heads, relations, tails, packed, rows, ids, sems):
    sources = (features, heads, relations, tails)
    targets = (rows, ids.at[0], ids.at[1], ids.at[2])
    copies = [
        pltpu.make_async_copy(source, target, sems.at[i])
        for i, (source, target) in enumerate(zip(sources, targets, strict=True))
    ]
    for copy in copies:
        copy.start()
    for copy in copies:
        copy.wait()
    width = features.shape[1]
    packed[:, :width] = rows[...]
    columns = [ids[0], ids[2], ids[1] // LANES, ids[1] % LANES]
    packed[:, width:] = jnp.concatenate(columns, axis=0).astype(F32).astype(BF16)


def pick_kernel(rows, offset, skipped, block, table, *rest):
    picked, ids = rest[-2:]
    ids[...] = block[:, block.shape[1] - LANES :].astype(F32)
    me = lax.axis_index("grp").astype(jnp.int32)
    count = block.shape[0] // rows
    pick_blocks(ids, range(skipped, count), me, rows, table, picked.at[pl.ds(offset, count)])


def sigmoid_parts(value):
    small = jnp.exp(-jnp.abs(value))
    softplus = jnp.maximum(value, 0.0) + jnp.log(1.0 + small)
    sigmoid = jnp.where(value >= 0.0, 1.0, small) / (1.0 + small)
    return softplus, sigmoid


def score_kernel(
    rows,
    keys,
    partner,
    mine,
    other,
    w_first,
    w_second,
    table,
    negatives,
    picked_mine,
    picked_early,
    grad_out,
    loss_out,
    slope_out,
    hidden_out,
    encoded,
    ids,
    grads,
    picked_other,
    scores_kept,
    weights_kept,
    partner_kept,
    partner_sem,
):
    fetch = pltpu.make_async_copy(partner, partner_kept, partner_sem)
    fetch.start()
    width = w_first.shape[0]
    half = encoded.shape[1] // 2
    places = len(keys)
    all_rows = places * rows
    group_rows = 2 * rows
    members = (0, all_rows)
    me = lax.axis_index("grp").astype(jnp.int32)

    ids[:all_rows, :] = mine[:, width:].astype(F32)
    ids[all_rows:, :] = other[:, width:].astype(F32)
    features = jnp.concatenate([mine[:, :width], other[:, :width]], axis=0)
    pre_act = jnp.dot(features, w_first[...], preferred_element_type=F32)
    gate = 1.0 / (1.0 + jnp.exp(-pre_act))
    hidden = (pre_act * gate).astype(BF16)
    slope_out[...] = gate * (1.0 + pre_act * (1.0 - gate))
    hidden_out[...] = hidden
    encoded[...] = jnp.dot(hidden, w_second[...], preferred_element_type=F32).astype(BF16).astype(F32)
    early = picked_early.shape[0]
    picked_other[:early] = picked_early[...]
    pick_blocks(ids.at[pl.ds(all_rows, all_rows)], range(early, places), me, rows, table, picked_other)

    labels = [(i ^ (me * rows)).astype(F32) for i in range(group_rows)]
    label_column = lax.broadcasted_iota(jnp.int32, (group_rows, 1), 0) ^ (me * rows)
    drawn = negatives[pl.ds(me, 1), :]
    counts = jnp.sum((drawn == label_column).astype(F32), axis=1, keepdims=True)
    negative_count = negatives.shape[1]
    label_column = label_column.astype(F32)
    fetch.wait()
    far_place = place_of(partner_kept[me, 0], keys)
    low_bit = far_place & -far_place

    def edge_ids(kind, place):
        return jnp.concatenate(
            [id_row(ids.at[pl.ds(base, all_rows)], kind, place, me, rows) for base in members], axis=1
        )

    def group_of(place):
        return jnp.concatenate(
            [encoded[pl.ds(pl.multiple_of(base + place * rows, rows), rows), :] for base in members],
            axis=0,
        )

    def relations_of(place):
        return jnp.concatenate([picked_mine[place], picked_other[place]], axis=1)

    for place in range(places):
        near_rows, far_rows = group_of(place), group_of(place ^ far_place)
        near_re, near_im = near_rows[:, :half], near_rows[:, half:]
        far_re, far_im = far_rows[:, :half], far_rows[:, half:]
        pairs = jnp.concatenate(
            [
                jnp.concatenate(
                    [
                        near_re[i : i + 1] * far_re + near_im[i : i + 1] * far_im,
                        near_re[i : i + 1] * far_im - near_im[i : i + 1] * far_re,
                    ],
                    axis=1,
                ).astype(BF16)
                for i in range(group_rows)
            ],
            axis=0,
        )
        scores = jnp.dot(pairs, relations_of(place), preferred_element_type=F32)
        head = edge_ids(HEAD, place)
        negative = jnp.zeros((group_rows, scores.shape[1]), F32)
        for i in range(group_rows):
            negative = jnp.where(
                head == labels[i], scores[i * group_rows : (i + 1) * group_rows], negative
            )
        scores_kept[place] = negative

    for place in range(places):
        negative = scores_kept[place]
        is_tail = edge_ids(TAIL, place) == label_column
        positive = jnp.sum(jnp.where(is_tail, negative, 0.0), axis=0, keepdims=True)
        loss, chance = sigmoid_parts(negative)
        loss_positive, chance_positive = sigmoid_parts(-positive)
        if place == 0:
            loss_out[...] = loss_positive + jnp.sum(loss * counts, axis=0, keepdims=True) / negative_count
        weight = (chance / negative_count).astype(BF16).astype(F32) * counts
        weights_kept[place] = (weight - jnp.where(is_tail, chance_positive, 0.0)).astype(BF16)

    for pair in range(places // 2):
        place = pair + (pair & -low_bit)
        far = place ^ far_place
        near_weight, far_weight = weights_kept[place], weights_kept[far]
        near_head, far_head = edge_ids(HEAD, place), edge_ids(HEAD, far)
        far_hot = (far_head == label_column).astype(BF16)
        near_rows, far_rows = group_of(place), group_of(far)
        near_re, near_im = near_rows[:, :half], near_rows[:, half:]
        far_re, far_im = far_rows[:, :half], far_rows[:, half:]
        weights = jnp.concatenate(
            [
                jnp.concatenate(
                    [near_weight * (near_head == labels[i]).astype(BF16), far_weight[i : i + 1] * far_hot],
                    axis=1,
                )
                for i in range(group_rows)
            ],
            axis=0,
        )
        relation = relations_of(place)
        relation = jnp.concatenate([relation[:half], -relation[half:]], axis=0)
        joint = lax.dot_general(
            weights,
            jnp.concatenate([relation, relations_of(far)], axis=1),
            (((1,), (1,)), ((), ())),
            preferred_element_type=F32,
        )
        far_grad_re = jnp.zeros((group_rows, half), F32)
        far_grad_im = jnp.zeros((group_rows, half), F32)
        near_grad = []
        for i in range(group_rows):
            part_re = joint[i * group_rows : (i + 1) * group_rows, :half]
            part_im = joint[i * group_rows : (i + 1) * group_rows, half:]
            row_re, row_im = near_re[i : i + 1], near_im[i : i + 1]
            far_grad_re = far_grad_re + (row_re * part_re + row_im * part_im)
            far_grad_im = far_grad_im + (row_im * part_re - row_re * part_im)
            near_grad.append(
                jnp.concatenate(
                    [
                        jnp.sum(far_re * part_re - far_im * part_im, axis=0, keepdims=True),
                        jnp.sum(far_im * part_re + far_re * part_im, axis=0, keepdims=True),
                    ],
                    axis=1,
                )
            )
        near_grad = jnp.concatenate(near_grad, axis=0)
        far_grad = jnp.concatenate([far_grad_re, far_grad_im], axis=1)
        for member, base in enumerate(members):
            span = slice(member * rows, (member + 1) * rows)
            grads[pl.ds(pl.multiple_of(base + place * rows, rows), rows), :] = near_grad[span]
            grads[pl.ds(pl.multiple_of(base + far * rows, rows), rows), :] = far_grad[span]
    grad_out[...] = grads[...].astype(BF16)


def total_kernel(
    limit,
    mine,
    other,
    grad_mine,
    grad_other,
    slope,
    hidden,
    w_second,
    loss_mine,
    loss_other,
    loss_out,
    first_out,
    second_out,
):
    me = lax.axis_index("grp").astype(jnp.int32)
    all_rows = mine.shape[0]
    grad = jnp.concatenate(
        [
            grad_mine[:all_rows].astype(F32) + grad_other[all_rows:].astype(F32),
            grad_mine[all_rows:].astype(F32) + grad_other[:all_rows].astype(F32),
        ],
        axis=0,
    ).astype(BF16)
    across = (((0,), (0,)), ((), ()))
    grad_hidden = lax.dot_general(
        grad, w_second[...], (((1,), (1,)), ((), ())), preferred_element_type=F32
    )
    grad_pre = (grad_hidden * slope[...]).astype(BF16)
    squares = jnp.zeros((1, 1), F32)
    for target, parts, factor in ((second_out, (hidden,), grad), (first_out, (mine, other), grad_pre)):
        share = target.shape[0]
        for member in (me, 1 - me):
            columns = pl.ds(pl.multiple_of(member * share, share), share)
            rows = jnp.concatenate([part[:, columns] for part in parts], axis=0)
            total = lax.dot_general(rows, factor, across, preferred_element_type=F32)
            squares = squares + jnp.sum(total * total, axis=(0, 1), keepdims=True)
            if member is me:
                target[...] = total
    factor = jnp.minimum(1.0, limit / jnp.sqrt(squares + 1e-06))
    first_out[...] = first_out[...] * factor
    second_out[...] = second_out[...] * factor
    edges = loss_out.shape[1]
    for member in range(2):
        loss_out[pl.ds(member, 1), :] = jnp.where(
            me == member, loss_mine[:, :edges], loss_other[:, edges:]
        )


def kernel_call(body, name, out_shape, scratch=(), flops=0, spaces=None, mebibytes=20, **more):
    vmem = pl.BlockSpec(memory_space=pltpu.VMEM)
    in_specs = None if spaces is None else [pl.BlockSpec(memory_space=space) for space in spaces]
    return pl.pallas_call(
        body,
        out_shape=out_shape,
        in_specs=in_specs,
        out_specs=jax.tree.map(lambda _: vmem, out_shape),
        scratch_shapes=scratch,
        compiler_params=pltpu.CompilerParams(vmem_limit_bytes=mebibytes * 1024 * 1024),
        cost_estimate=pl.CostEstimate(flops=flops, bytes_accessed=0, transcendentals=0),
        name=name,
        **more,
    )


def together(
    features, w_first, w_second, relation_table, heads, relations, tails, negatives, partner
):
    rows, width = features.shape
    rounds, edges = heads.shape
    hidden_width, encoded_width = w_second.shape
    size = lax.axis_size("dom")
    keys = keys_of(size)
    steps = distances_of(size)
    all_rows = 2 * size * rows
    shape = jax.ShapeDtypeStruct
    table = jnp.pad(relation_table.T, ((0, 0), (0, -relation_table.shape[0] % LANES)))
    picked_shape = shape((size, encoded_width, edges), BF16)
    flops = 2 * table.size * edges

    block = kernel_call(
        pack_kernel,
        "pack",
        shape((rows, width + edges), BF16),
        [
            pltpu.VMEM(features.shape, BF16),
            pltpu.VMEM((3, rounds, edges), jnp.int32),
            pltpu.SemaphoreType.DMA((4,)),
        ],
        spaces=[pltpu.HBM] * 4,
        mebibytes=60,
    )(features, heads, relations, tails)
    for step in steps[:-1]:
        block, table = join(block, arrivals(block, "dom", step), table)
    early = block.shape[0] // rows

    def pick(block, count, *begun, offset=0, skipped=0):
        places = block.shape[0] // rows
        return kernel_call(
            functools.partial(pick_kernel, rows, offset, skipped),
            "pick",
            shape((count, encoded_width, edges), BF16),
            [pltpu.VMEM((places * rows, edges), F32)],
            flops * (places - skipped),
            [pltpu.VMEM] * (2 + len(begun)),
            input_output_aliases={2: 0} if begun else {},
        )(block, table, *begun)

    early_ids = swap(block[:, width:], "grp", 1)
    arrived = arrivals(block, "dom", steps[-1])
    picked = pick(block, size)
    picked_early = pick(early_ids, early)
    picked = pick(arrived[0], size, picked, offset=early)
    mine, picked, picked_early = join(block, arrived, picked, picked_early)
    picked = pick(mine, size, picked, skipped=2 * early)
    other = swap(mine, "grp", 1)

    grad, loss, slope, hidden = kernel_call(
        functools.partial(score_kernel, rows, keys),
        "scores",
        (
            shape((all_rows, encoded_width), BF16),
            shape((1, 2 * edges), F32),
            shape((all_rows, hidden_width), F32),
            shape((all_rows, hidden_width), BF16),
        ),
        [
            pltpu.VMEM((all_rows, encoded_width), F32),
            pltpu.VMEM((all_rows, edges), F32),
            pltpu.VMEM((all_rows, encoded_width), F32),
            pltpu.VMEM(picked_shape.shape, BF16),
            pltpu.VMEM((size, 2 * rows, 2 * edges), F32),
            pltpu.VMEM((size, 2 * rows, 2 * edges), BF16),
            pltpu.SMEM(partner.shape, jnp.int32),
            pltpu.SemaphoreType.DMA,
        ],
        flops * size * 2,
        [pl.ANY] + [pltpu.VMEM] * 8,
    )(partner, mine, other, w_first, w_second, table, negatives, picked, picked_early)
    grad_other = swap(grad, "grp", 1)
    loss_other = swap(loss, "grp", 1)
    return kernel_call(
        functools.partial(total_kernel, math.sqrt(w_first.size + w_second.size)),
        "totals",
        (
            shape((rounds, edges), F32),
            shape((w_first.shape[0] // 2, w_first.shape[1]), F32),
            shape((w_second.shape[0] // 2, w_second.shape[1]), F32),
        ),
        spaces=[pltpu.VMEM] * 9,
    )(mine, other, grad, grad_other, slope, hidden, w_second, loss, loss_other)


def solution(mesh):
    def per_device(features, w_first, w_second, relation_table, heads, relations, tails, *rest):
        rounds, edges = heads.shape
        rows = features.shape[0]
        fits = (
            mesh.shape["grp"] == rounds == ROUNDS == 2
            and edges == LANES
            and 4 * rounds == rows
            and mesh.shape["dom"] >= 8
        )
        plan = together if fits else spread
        return plan(features, w_first, w_second, relation_table, heads, relations, tails, *rest)

    return jax.shard_map(
        per_device,
        mesh=mesh,
        in_specs=(
            P(("dom", "grp"), None),
            P(),
            P(),
            P(),
            P(None, ("dom", "grp")),
            P(None, ("dom", "grp")),
            P(None, ("dom", "grp")),
            P(),
            P(),
        ),
        out_specs=(P(None, ("dom", "grp")), P("grp", None), P("grp", None)),
        check_vma=False,
    )
```

```python
import functools
import math

import jax
import jax.numpy as jnp
from jax import lax
from jax.experimental import pallas as pl
from jax.experimental.pallas import tpu as pltpu
from jax.sharding import PartitionSpec as P

LANES = 128
F32 = jnp.float32
BF16 = jnp.bfloat16


def partner_2(value, axis, distance):
    return lax.ppermute(value, axis, [(i, i ^ 1 << distance) for i in range(lax.axis_size(axis))])


def encode(rows, w_first, w_second):
    pre_act = jnp.dot(rows, w_first, preferred_element_type=jnp.float32)
    hidden = jax.nn.silu(pre_act).astype(jnp.bfloat16)
    encoded = jnp.dot(hidden, w_second, preferred_element_type=jnp.float32).astype(jnp.bfloat16)
    return (pre_act, hidden, encoded)


def backward(rows, pre_act, hidden, grad_rows, w_second):
    term_second = lax.dot_general(
        hidden, grad_rows, (((0,), (0,)), ((), ())), preferred_element_type=jnp.float32
    )
    grad_hidden = lax.dot_general(
        grad_rows, w_second, (((1,), (1,)), ((), ())), preferred_element_type=jnp.float32
    )
    sigmoid_pre = jax.nn.sigmoid(pre_act)
    silu_slope = sigmoid_pre * (1.0 + pre_act * (1.0 - sigmoid_pre))
    grad_pre = (grad_hidden * silu_slope).astype(jnp.bfloat16)
    term_first = lax.dot_general(
        rows, grad_pre, (((0,), (0,)), ((), ())), preferred_element_type=jnp.float32
    )
    return (term_first, term_second)


def row_select(ids, row_count):
    return ids[:, None] == jnp.arange(row_count, dtype=jnp.int32)[None, :]


def pick_rows(selector, table):
    return jnp.dot(selector.astype(jnp.bfloat16), table, preferred_element_type=jnp.float32)


def add_into_rows(selector, values):
    return lax.dot_general(
        selector.astype(jnp.float32),
        values,
        (((0,), (0,)), ((), ())),
        precision=lax.Precision.HIGHEST,
        preferred_element_type=jnp.float32,
    )


def score_block(own, other, relation_table, head_ids, relation_ids, tail_ids, negative_ids):
    half_width = own.shape[1] // 2
    row_count = own.shape[0]
    head_select = row_select(head_ids, row_count)
    tail_select = row_select(tail_ids, row_count)
    negative_select = row_select(negative_ids, row_count)
    head_rows = pick_rows(head_select, own)
    rel_rows = jnp.take(relation_table, relation_ids, axis=0).astype(jnp.float32)
    tail_rows = pick_rows(tail_select, other)
    negative_rows = pick_rows(negative_select, other).astype(jnp.bfloat16)
    head_real, head_imag = (head_rows[:, :half_width], head_rows[:, half_width:])
    rel_real, rel_imag = (rel_rows[:, :half_width], rel_rows[:, half_width:])
    query = jnp.concatenate(
        [head_real * rel_real - head_imag * rel_imag, head_real * rel_imag + head_imag * rel_real],
        axis=1,
    ).astype(jnp.bfloat16)
    query_wide = query.astype(jnp.float32)
    positive = jnp.sum(query_wide * tail_rows, axis=1)
    negative = lax.dot_general(
        query, negative_rows, (((1,), (1,)), ((), ())), preferred_element_type=jnp.float32
    )
    edge_loss = (
        jax.nn.softplus(-positive) + jnp.sum(jax.nn.softplus(negative), axis=1) / negative.shape[1]
    )
    weight_neg = (jax.nn.sigmoid(negative) / negative.shape[1]).astype(jnp.bfloat16)
    weight_pos = -jax.nn.sigmoid(-positive)
    grad_query = weight_pos[:, None] * tail_rows + jnp.dot(
        weight_neg, negative_rows, preferred_element_type=jnp.float32
    )
    grad_tail = weight_pos[:, None] * query_wide
    grad_negative = lax.dot_general(
        weight_neg, query, (((0,), (0,)), ((), ())), preferred_element_type=jnp.float32
    )
    grad_real, grad_imag = (grad_query[:, :half_width], grad_query[:, half_width:])
    grad_head = jnp.concatenate(
        [grad_real * rel_real + grad_imag * rel_imag, grad_imag * rel_real - grad_real * rel_imag],
        axis=1,
    )
    own_part = add_into_rows(head_select, grad_head)
    far_part = add_into_rows(tail_select, grad_tail) + add_into_rows(negative_select, grad_negative)
    return (edge_loss, own_part, far_part)


def route_rows(payload, xor_mask, bit_count, mover):
    for bit_level in range(bit_count):
        swapped = mover(payload, bit_level)
        payload = jnp.where(xor_mask >> bit_level & 1 == 1, swapped, payload)
    return payload


def spread(
    features, w_first, w_second, relation_table, heads, relations, tails, negatives, partner
):
    pre_act, hidden, encoded = encode(features, w_first, w_second)
    own_block = lax.all_gather(encoded, "grp", axis=0, tiled=True)
    bit_count = lax.axis_size("dom").bit_length() - 1
    total_first = jnp.zeros(w_first.shape, jnp.float32)
    total_second = jnp.zeros(w_second.shape, jnp.float32)
    own_acc = jnp.zeros(own_block.shape, jnp.float32)
    losses = []
    for bucket in range(heads.shape[0]):
        xor_mask = partner[bucket, 0]
        arrived = route_rows(
            encoded,
            xor_mask,
            bit_count,
            lambda payload, bit_level: partner_2(payload, "dom", bit_level),
        )
        far_block = lax.all_gather(arrived, "grp", axis=0, tiled=True)
        edge_loss, own_part, far_part = score_block(
            own_block,
            far_block,
            relation_table,
            heads[bucket],
            relations[bucket],
            tails[bucket],
            negatives[bucket],
        )
        losses.append(edge_loss)
        own_acc = own_acc + own_part
        far_grad = lax.psum_scatter(
            far_part.astype(jnp.bfloat16), "grp", scatter_dimension=0, tiled=True
        )
        returned = route_rows(
            far_grad,
            xor_mask,
            bit_count,
            lambda payload, bit_level: partner_2(payload, "dom", bit_level),
        )
        term_first, term_second = backward(features, pre_act, hidden, returned, w_second)
        total_first = total_first + term_first
        total_second = total_second + term_second
    own_grad = lax.psum_scatter(
        own_acc.astype(jnp.bfloat16), "grp", scatter_dimension=0, tiled=True
    )
    term_first, term_second = backward(features, pre_act, hidden, own_grad, w_second)
    total_first = total_first + term_first
    total_second = total_second + term_second
    part_first, part_second = (
        lax.psum_scatter(
            total_first.astype(jnp.bfloat16), "grp", scatter_dimension=0, tiled=True
        ).astype(jnp.float32),
        lax.psum_scatter(
            total_second.astype(jnp.bfloat16), "grp", scatter_dimension=0, tiled=True
        ).astype(jnp.float32),
    )
    summed_first, summed_second = lax.psum((part_first, part_second), "dom")
    local_squares = jnp.sum(summed_first * summed_first) + jnp.sum(summed_second * summed_second)
    squares = lax.psum(local_squares, "grp")
    factor = jnp.minimum(1.0, math.sqrt(w_first.size + w_second.size) / jnp.sqrt(squares + 1e-06))
    return (jnp.stack(losses), summed_first * factor, summed_second * factor)


ROUNDS = 2
HEAD, TAIL, HIGH, LOW = 0, 1, 2, 3
LANE_BITS = LANES.bit_length() - 1


def swap(value, axis, distance):
    return lax.ppermute(value, axis, [(i, i ^ distance) for i in range(lax.axis_size(axis))])


def distances_of(size):
    steps = []
    while size > 1:
        radix = min(size, 4)
        size //= radix
        steps.append([i * size for i in range(radix - 1, 0, -1)])
    return steps


def arrivals(value, axis, step):
    return [swap(value, axis, distance) for distance in step]


def join(value, arrived, *beside):
    count = len(arrived)
    done = lax.optimization_barrier((*arrived, *beside))
    return jnp.concatenate([value, *done[:count]], axis=0), *done[count:]


def keys_of(size):
    keys = [0]
    for step in distances_of(size):
        keys = keys + [key ^ distance for distance in step for key in keys]
    return keys


def place_of(mask, keys):
    place, bit = jnp.int32(0), 1
    while bit < len(keys):
        place = place ^ jnp.where((mask & bit) != 0, keys.index(bit), 0)
        bit *= 2
    return place


def id_row(ids, kind, place, me, rows):
    return ids[pl.ds(place * rows + kind * ROUNDS + me, 1), :]


def pick_relations(low, high, table):
    low_column = lax.broadcasted_iota(jnp.int32, (LANES, 1), 0).astype(F32)
    low_hot = (low == low_column).astype(BF16)
    hot = jnp.concatenate(
        [low_hot * (high == float(block)).astype(BF16) for block in range(table.shape[1] // LANES)],
        axis=0,
    )
    columns = jnp.dot(table[...], hot, preferred_element_type=F32).astype(BF16)
    return columns[:, :LANES], columns[:, LANES:]


def pick_blocks(ids, places, me, rows, table, picked):
    for first in range(places.start, places.stop, 2):
        low, high = [
            jnp.concatenate([id_row(ids, kind, place, me, rows) for place in (first, first + 1)], axis=1)
            for kind in (LOW, HIGH)
        ]
        picked[first], picked[first + 1] = pick_relations(low, high, table)


def pack(features, heads, tails, relations):
    rows, width = features.shape

    def placed(value, top, left):
        beyond = rows - top - value.shape[0], width + LANES - left - value.shape[1]
        return lax.pad(value, jnp.zeros((), value.dtype), ((top, beyond[0], 0), (left, beyond[1], 0)))

    kinds = ((HEAD, heads), (TAIL, tails), (HIGH, relations))
    ids = sum(placed(value, kind * ROUNDS, width) for kind, value in kinds)
    both = placed(features, 0, 0).astype(F32) + ids.astype(F32)
    both = lax.optimization_barrier(both)
    ids = both[:, width:]
    high = jnp.floor(ids[HIGH * ROUNDS : LOW * ROUNDS] * (1.0 / LANES))
    low = ids[HIGH * ROUNDS : LOW * ROUNDS] - high * LANES
    ids = jnp.concatenate([ids[: HIGH * ROUNDS], high, low], axis=0)
    return jnp.concatenate([both[:, :width], ids], axis=1).astype(BF16)


def pick_kernel(rows, offset, skipped, block, table, *rest):
    picked, ids = rest[-2:]
    ids[...] = block[:, block.shape[1] - LANES :].astype(F32)
    me = lax.axis_index("grp").astype(jnp.int32)
    count = block.shape[0] // rows
    pick_blocks(ids, range(skipped, count), me, rows, table, picked.at[pl.ds(offset, count)])


def sigmoid_parts(value):
    small = jnp.exp(-jnp.abs(value))
    softplus = jnp.maximum(value, 0.0) + jnp.log(1.0 + small)
    sigmoid = jnp.where(value >= 0.0, 1.0, small) / (1.0 + small)
    return softplus, sigmoid


def score_kernel(
    rows,
    keys,
    partner,
    mine,
    other,
    w_first,
    w_second,
    table,
    negatives,
    picked_mine,
    picked_early,
    grad_out,
    loss_out,
    slope_out,
    hidden_out,
    encoded,
    ids,
    grads,
    picked_other,
    scores_kept,
    weights_kept,
    partner_kept,
    partner_sem,
):
    fetch = pltpu.make_async_copy(partner, partner_kept, partner_sem)
    fetch.start()
    width = w_first.shape[0]
    half = encoded.shape[1] // 2
    places = len(keys)
    all_rows = places * rows
    group_rows = 2 * rows
    members = (0, all_rows)
    me = lax.axis_index("grp").astype(jnp.int32)

    ids[:all_rows, :] = mine[:, width:].astype(F32)
    ids[all_rows:, :] = other[:, width:].astype(F32)
    features = jnp.concatenate([mine[:, :width], other[:, :width]], axis=0)
    pre_act = jnp.dot(features, w_first[...], preferred_element_type=F32)
    gate = 1.0 / (1.0 + jnp.exp(-pre_act))
    hidden = (pre_act * gate).astype(BF16)
    slope_out[...] = gate * (1.0 + pre_act * (1.0 - gate))
    hidden_out[...] = hidden
    encoded[...] = jnp.dot(hidden, w_second[...], preferred_element_type=F32).astype(BF16).astype(F32)
    early = picked_early.shape[0]
    picked_other[:early] = picked_early[...]
    pick_blocks(ids.at[pl.ds(all_rows, all_rows)], range(early, places), me, rows, table, picked_other)

    labels = [(i ^ (me * rows)).astype(F32) for i in range(group_rows)]
    label_column = lax.broadcasted_iota(jnp.int32, (group_rows, 1), 0) ^ (me * rows)
    drawn = negatives[pl.ds(me, 1), :]
    counts = jnp.sum((drawn == label_column).astype(F32), axis=1, keepdims=True)
    negative_count = negatives.shape[1]
    label_column = label_column.astype(F32)
    fetch.wait()
    far_place = place_of(partner_kept[me, 0], keys)
    low_bit = far_place & -far_place

    def edge_ids(kind, place):
        return jnp.concatenate(
            [id_row(ids.at[pl.ds(base, all_rows)], kind, place, me, rows) for base in members], axis=1
        )

    def group_of(place):
        return jnp.concatenate(
            [encoded[pl.ds(pl.multiple_of(base + place * rows, rows), rows), :] for base in members],
            axis=0,
        )

    def relations_of(place):
        return jnp.concatenate([picked_mine[place], picked_other[place]], axis=1)

    for place in range(places):
        near_rows, far_rows = group_of(place), group_of(place ^ far_place)
        near_re, near_im = near_rows[:, :half], near_rows[:, half:]
        far_re, far_im = far_rows[:, :half], far_rows[:, half:]
        pairs = jnp.concatenate(
            [
                jnp.concatenate(
                    [
                        near_re[i : i + 1] * far_re + near_im[i : i + 1] * far_im,
                        near_re[i : i + 1] * far_im - near_im[i : i + 1] * far_re,
                    ],
                    axis=1,
                ).astype(BF16)
                for i in range(group_rows)
            ],
            axis=0,
        )
        scores = jnp.dot(pairs, relations_of(place), preferred_element_type=F32)
        head = edge_ids(HEAD, place)
        negative = jnp.zeros((group_rows, scores.shape[1]), F32)
        for i in range(group_rows):
            negative = jnp.where(
                head == labels[i], scores[i * group_rows : (i + 1) * group_rows], negative
            )
        scores_kept[place] = negative

    for place in range(places):
        negative = scores_kept[place]
        is_tail = edge_ids(TAIL, place) == label_column
        positive = jnp.sum(jnp.where(is_tail, negative, 0.0), axis=0, keepdims=True)
        loss, chance = sigmoid_parts(negative)
        loss_positive, chance_positive = sigmoid_parts(-positive)
        if place == 0:
            loss_out[...] = loss_positive + jnp.sum(loss * counts, axis=0, keepdims=True) / negative_count
        weight = (chance / negative_count).astype(BF16).astype(F32) * counts
        weights_kept[place] = (weight - jnp.where(is_tail, chance_positive, 0.0)).astype(BF16)

    sublane = lax.broadcasted_iota(jnp.int32, (rows, half), 0)

    def halved(value):
        return value[:rows] + value[rows:]

    def row_sums(blocks):
        step = 1
        while len(blocks) > 1:
            upper = (sublane & step) != 0
            blocks = [
                jnp.where(upper, second, first) + pltpu.roll(jnp.where(upper, first, second), step, 0)
                for first, second in zip(blocks[::2], blocks[1::2], strict=True)
            ]
            step *= 2
        return blocks[0]

    for pair in range(places // 2):
        place = pair + (pair & -low_bit)
        far = place ^ far_place
        near_weight, far_weight = weights_kept[place], weights_kept[far]
        near_head, far_head = edge_ids(HEAD, place), edge_ids(HEAD, far)
        far_hot = (far_head == label_column).astype(BF16)
        near_rows, far_rows = group_of(place), group_of(far)
        near_re, near_im = near_rows[:, :half], near_rows[:, half:]
        far_re, far_im = far_rows[:, :half], far_rows[:, half:]
        weights = jnp.concatenate(
            [
                jnp.concatenate(
                    [near_weight * (near_head == labels[i]).astype(BF16), far_weight[i : i + 1] * far_hot],
                    axis=1,
                )
                for i in range(group_rows)
            ],
            axis=0,
        )
        relation = relations_of(place)
        relation = jnp.concatenate([relation[:half], -relation[half:]], axis=0)
        joint = lax.dot_general(
            weights,
            jnp.concatenate([relation, relations_of(far)], axis=1),
            (((1,), (1,)), ((), ())),
            preferred_element_type=F32,
        )
        far_grad_re = jnp.zeros((group_rows, half), F32)
        far_grad_im = jnp.zeros((group_rows, half), F32)
        near_grad = []
        for i in range(group_rows):
            part_re = joint[i * group_rows : (i + 1) * group_rows, :half]
            part_im = joint[i * group_rows : (i + 1) * group_rows, half:]
            row_re, row_im = near_re[i : i + 1], near_im[i : i + 1]
            far_grad_re = far_grad_re + (row_re * part_re + row_im * part_im)
            far_grad_im = far_grad_im + (row_im * part_re - row_re * part_im)
            near_grad.append(
                (
                    halved(far_re * part_re - far_im * part_im),
                    halved(far_im * part_re + far_re * part_im),
                )
            )
        near_grad = jnp.concatenate(
            [
                jnp.concatenate([row_sums([part[k] for part in near_grad[i : i + rows]]) for k in (0, 1)], axis=1)
                for i in range(0, group_rows, rows)
            ],
            axis=0,
        )
        far_grad = jnp.concatenate([far_grad_re, far_grad_im], axis=1)
        for member, base in enumerate(members):
            span = slice(member * rows, (member + 1) * rows)
            grads[pl.ds(pl.multiple_of(base + place * rows, rows), rows), :] = near_grad[span]
            grads[pl.ds(pl.multiple_of(base + far * rows, rows), rows), :] = far_grad[span]
    grad_out[...] = grads[...].astype(BF16)


def total_kernel(
    limit,
    mine,
    other,
    grad_mine,
    grad_other,
    slope,
    hidden,
    w_second,
    loss_mine,
    loss_other,
    loss_out,
    first_out,
    second_out,
):
    me = lax.axis_index("grp").astype(jnp.int32)
    all_rows = mine.shape[0]
    grad = jnp.concatenate(
        [
            grad_mine[:all_rows].astype(F32) + grad_other[all_rows:].astype(F32),
            grad_mine[all_rows:].astype(F32) + grad_other[:all_rows].astype(F32),
        ],
        axis=0,
    ).astype(BF16)
    across = (((0,), (0,)), ((), ()))
    grad_hidden = lax.dot_general(
        grad, w_second[...], (((1,), (1,)), ((), ())), preferred_element_type=F32
    )
    grad_pre = (grad_hidden * slope[...]).astype(BF16)
    squares = jnp.zeros((1, 1), F32)
    for target, parts, factor in ((second_out, (hidden,), grad), (first_out, (mine, other), grad_pre)):
        share = target.shape[0]
        for member in (me, 1 - me):
            columns = pl.ds(pl.multiple_of(member * share, share), share)
            rows = jnp.concatenate([part[:, columns] for part in parts], axis=0)
            total = lax.dot_general(rows, factor, across, preferred_element_type=F32)
            squares = squares + jnp.sum(total * total, axis=(0, 1), keepdims=True)
            if member is me:
                target[...] = total
    factor = jnp.minimum(1.0, limit / jnp.sqrt(squares + 1e-06))
    first_out[...] = first_out[...] * factor
    second_out[...] = second_out[...] * factor
    edges = loss_out.shape[1]
    for member in range(2):
        loss_out[pl.ds(member, 1), :] = jnp.where(
            me == member, loss_mine[:, :edges], loss_other[:, edges:]
        )


def kernel_call(body, name, out_shape, scratch=(), flops=0, spaces=None, mebibytes=20, **more):
    vmem = pl.BlockSpec(memory_space=pltpu.VMEM)
    in_specs = None if spaces is None else [pl.BlockSpec(memory_space=space) for space in spaces]
    return pl.pallas_call(
        body,
        out_shape=out_shape,
        in_specs=in_specs,
        out_specs=jax.tree.map(lambda _: vmem, out_shape),
        scratch_shapes=scratch,
        compiler_params=pltpu.CompilerParams(vmem_limit_bytes=mebibytes * 1024 * 1024),
        cost_estimate=pl.CostEstimate(flops=flops, bytes_accessed=0, transcendentals=0),
        name=name,
        **more,
    )


def together(
    features, w_first, w_second, relation_table, heads, relations, tails, negatives, partner
):
    rows, width = features.shape
    rounds, edges = heads.shape
    hidden_width, encoded_width = w_second.shape
    size = lax.axis_size("dom")
    keys = keys_of(size)
    steps = distances_of(size)
    all_rows = 2 * size * rows
    shape = jax.ShapeDtypeStruct
    table = jnp.pad(relation_table.T, ((0, 0), (0, -relation_table.shape[0] % LANES)))
    picked_shape = shape((size, encoded_width, edges), BF16)
    flops = 2 * table.size * edges

    block = pack(features, heads, tails, relations)
    for step in steps[:-1]:
        block, table = join(block, arrivals(block, "dom", step), table)
    early = block.shape[0] // rows

    def pick(block, count, *begun, offset=0, skipped=0):
        places = block.shape[0] // rows
        return kernel_call(
            functools.partial(pick_kernel, rows, offset, skipped),
            "pick",
            shape((count, encoded_width, edges), BF16),
            [pltpu.VMEM((places * rows, edges), F32)],
            flops * (places - skipped),
            [pltpu.VMEM] * (2 + len(begun)),
            input_output_aliases={2: 0} if begun else {},
        )(block, table, *begun)

    early_ids = swap(block[:, width:], "grp", 1)
    arrived = arrivals(block, "dom", steps[-1])
    picked = pick(block, size)
    picked_early = pick(early_ids, early)
    picked = pick(arrived[0], size, picked, offset=early)
    mine, picked, picked_early = join(block, arrived, picked, picked_early)
    picked = pick(mine, size, picked, skipped=2 * early)
    other = swap(mine, "grp", 1)

    grad, loss, slope, hidden = kernel_call(
        functools.partial(score_kernel, rows, keys),
        "scores",
        (
            shape((all_rows, encoded_width), BF16),
            shape((1, 2 * edges), F32),
            shape((all_rows, hidden_width), F32),
            shape((all_rows, hidden_width), BF16),
        ),
        [
            pltpu.VMEM((all_rows, encoded_width), F32),
            pltpu.VMEM((all_rows, edges), F32),
            pltpu.VMEM((all_rows, encoded_width), F32),
            pltpu.VMEM(picked_shape.shape, BF16),
            pltpu.VMEM((size, 2 * rows, 2 * edges), F32),
            pltpu.VMEM((size, 2 * rows, 2 * edges), BF16),
            pltpu.SMEM(partner.shape, jnp.int32),
            pltpu.SemaphoreType.DMA,
        ],
        flops * size * 2,
        [pl.ANY] + [pltpu.VMEM] * 8,
    )(partner, mine, other, w_first, w_second, table, negatives, picked, picked_early)
    grad_other = swap(grad, "grp", 1)
    loss_other = swap(loss, "grp", 1)
    return kernel_call(
        functools.partial(total_kernel, math.sqrt(w_first.size + w_second.size)),
        "totals",
        (
            shape((rounds, edges), F32),
            shape((w_first.shape[0] // 2, w_first.shape[1]), F32),
            shape((w_second.shape[0] // 2, w_second.shape[1]), F32),
        ),
        spaces=[pltpu.VMEM] * 9,
    )(mine, other, grad, grad_other, slope, hidden, w_second, loss, loss_other)


def solution(mesh):
    def per_device(features, w_first, w_second, relation_table, heads, relations, tails, *rest):
        rounds, edges = heads.shape
        rows = features.shape[0]
        fits = (
            mesh.shape["grp"] == rounds == ROUNDS == 2
            and edges == LANES
            and 4 * rounds == rows
            and mesh.shape["dom"] >= 8
            and relation_table.shape[0] <= LANES * 256
        )
        plan = together if fits else spread
        return plan(features, w_first, w_second, relation_table, heads, relations, tails, *rest)

    return jax.shard_map(
        per_device,
        mesh=mesh,
        in_specs=(
            P(("dom", "grp"), None),
            P(),
            P(),
            P(),
            P(None, ("dom", "grp")),
            P(None, ("dom", "grp")),
            P(None, ("dom", "grp")),
            P(),
            P(),
        ),
        out_specs=(P(None, ("dom", "grp")), P("grp", None), P("grp", None)),
        check_vma=False,
    )
```

```python
import functools
import math

import jax
import jax.numpy as jnp
from jax import lax
from jax.experimental import pallas as pl
from jax.experimental.pallas import tpu as pltpu
from jax.sharding import PartitionSpec as P

LANES = 128
F32 = jnp.float32
BF16 = jnp.bfloat16


def partner_2(value, axis, distance):
    return lax.ppermute(value, axis, [(i, i ^ 1 << distance) for i in range(lax.axis_size(axis))])


def encode(rows, w_first, w_second):
    pre_act = jnp.dot(rows, w_first, preferred_element_type=jnp.float32)
    hidden = jax.nn.silu(pre_act).astype(jnp.bfloat16)
    encoded = jnp.dot(hidden, w_second, preferred_element_type=jnp.float32).astype(jnp.bfloat16)
    return (pre_act, hidden, encoded)


def backward(rows, pre_act, hidden, grad_rows, w_second):
    term_second = lax.dot_general(
        hidden, grad_rows, (((0,), (0,)), ((), ())), preferred_element_type=jnp.float32
    )
    grad_hidden = lax.dot_general(
        grad_rows, w_second, (((1,), (1,)), ((), ())), preferred_element_type=jnp.float32
    )
    sigmoid_pre = jax.nn.sigmoid(pre_act)
    silu_slope = sigmoid_pre * (1.0 + pre_act * (1.0 - sigmoid_pre))
    grad_pre = (grad_hidden * silu_slope).astype(jnp.bfloat16)
    term_first = lax.dot_general(
        rows, grad_pre, (((0,), (0,)), ((), ())), preferred_element_type=jnp.float32
    )
    return (term_first, term_second)


def row_select(ids, row_count):
    return ids[:, None] == jnp.arange(row_count, dtype=jnp.int32)[None, :]


def pick_rows(selector, table):
    return jnp.dot(selector.astype(jnp.bfloat16), table, preferred_element_type=jnp.float32)


def add_into_rows(selector, values):
    return lax.dot_general(
        selector.astype(jnp.float32),
        values,
        (((0,), (0,)), ((), ())),
        precision=lax.Precision.HIGHEST,
        preferred_element_type=jnp.float32,
    )


def score_block(own, other, relation_table, head_ids, relation_ids, tail_ids, negative_ids):
    half_width = own.shape[1] // 2
    row_count = own.shape[0]
    head_select = row_select(head_ids, row_count)
    tail_select = row_select(tail_ids, row_count)
    negative_select = row_select(negative_ids, row_count)
    head_rows = pick_rows(head_select, own)
    rel_rows = jnp.take(relation_table, relation_ids, axis=0).astype(jnp.float32)
    tail_rows = pick_rows(tail_select, other)
    negative_rows = pick_rows(negative_select, other).astype(jnp.bfloat16)
    head_real, head_imag = (head_rows[:, :half_width], head_rows[:, half_width:])
    rel_real, rel_imag = (rel_rows[:, :half_width], rel_rows[:, half_width:])
    query = jnp.concatenate(
        [head_real * rel_real - head_imag * rel_imag, head_real * rel_imag + head_imag * rel_real],
        axis=1,
    ).astype(jnp.bfloat16)
    query_wide = query.astype(jnp.float32)
    positive = jnp.sum(query_wide * tail_rows, axis=1)
    negative = lax.dot_general(
        query, negative_rows, (((1,), (1,)), ((), ())), preferred_element_type=jnp.float32
    )
    edge_loss = (
        jax.nn.softplus(-positive) + jnp.sum(jax.nn.softplus(negative), axis=1) / negative.shape[1]
    )
    weight_neg = (jax.nn.sigmoid(negative) / negative.shape[1]).astype(jnp.bfloat16)
    weight_pos = -jax.nn.sigmoid(-positive)
    grad_query = weight_pos[:, None] * tail_rows + jnp.dot(
        weight_neg, negative_rows, preferred_element_type=jnp.float32
    )
    grad_tail = weight_pos[:, None] * query_wide
    grad_negative = lax.dot_general(
        weight_neg, query, (((0,), (0,)), ((), ())), preferred_element_type=jnp.float32
    )
    grad_real, grad_imag = (grad_query[:, :half_width], grad_query[:, half_width:])
    grad_head = jnp.concatenate(
        [grad_real * rel_real + grad_imag * rel_imag, grad_imag * rel_real - grad_real * rel_imag],
        axis=1,
    )
    own_part = add_into_rows(head_select, grad_head)
    far_part = add_into_rows(tail_select, grad_tail) + add_into_rows(negative_select, grad_negative)
    return (edge_loss, own_part, far_part)


def route_rows(payload, xor_mask, bit_count, mover):
    for bit_level in range(bit_count):
        swapped = mover(payload, bit_level)
        payload = jnp.where(xor_mask >> bit_level & 1 == 1, swapped, payload)
    return payload


def spread(
    features, w_first, w_second, relation_table, heads, relations, tails, negatives, partner
):
    pre_act, hidden, encoded = encode(features, w_first, w_second)
    own_block = lax.all_gather(encoded, "grp", axis=0, tiled=True)
    bit_count = lax.axis_size("dom").bit_length() - 1
    total_first = jnp.zeros(w_first.shape, jnp.float32)
    total_second = jnp.zeros(w_second.shape, jnp.float32)
    own_acc = jnp.zeros(own_block.shape, jnp.float32)
    losses = []
    for bucket in range(heads.shape[0]):
        xor_mask = partner[bucket, 0]
        arrived = route_rows(
            encoded,
            xor_mask,
            bit_count,
            lambda payload, bit_level: partner_2(payload, "dom", bit_level),
        )
        far_block = lax.all_gather(arrived, "grp", axis=0, tiled=True)
        edge_loss, own_part, far_part = score_block(
            own_block,
            far_block,
            relation_table,
            heads[bucket],
            relations[bucket],
            tails[bucket],
            negatives[bucket],
        )
        losses.append(edge_loss)
        own_acc = own_acc + own_part
        far_grad = lax.psum_scatter(
            far_part.astype(jnp.bfloat16), "grp", scatter_dimension=0, tiled=True
        )
        returned = route_rows(
            far_grad,
            xor_mask,
            bit_count,
            lambda payload, bit_level: partner_2(payload, "dom", bit_level),
        )
        term_first, term_second = backward(features, pre_act, hidden, returned, w_second)
        total_first = total_first + term_first
        total_second = total_second + term_second
    own_grad = lax.psum_scatter(
        own_acc.astype(jnp.bfloat16), "grp", scatter_dimension=0, tiled=True
    )
    term_first, term_second = backward(features, pre_act, hidden, own_grad, w_second)
    total_first = total_first + term_first
    total_second = total_second + term_second
    part_first, part_second = (
        lax.psum_scatter(
            total_first.astype(jnp.bfloat16), "grp", scatter_dimension=0, tiled=True
        ).astype(jnp.float32),
        lax.psum_scatter(
            total_second.astype(jnp.bfloat16), "grp", scatter_dimension=0, tiled=True
        ).astype(jnp.float32),
    )
    summed_first, summed_second = lax.psum((part_first, part_second), "dom")
    local_squares = jnp.sum(summed_first * summed_first) + jnp.sum(summed_second * summed_second)
    squares = lax.psum(local_squares, "grp")
    factor = jnp.minimum(1.0, math.sqrt(w_first.size + w_second.size) / jnp.sqrt(squares + 1e-06))
    return (jnp.stack(losses), summed_first * factor, summed_second * factor)


ROUNDS = 2
HEAD, TAIL, HIGH, LOW = 0, 1, 2, 3
LANE_BITS = LANES.bit_length() - 1


def swap(value, axis, distance):
    return lax.ppermute(value, axis, [(i, i ^ distance) for i in range(lax.axis_size(axis))])


def distances_of(size):
    steps = []
    while size > 1:
        radix = min(size, 4)
        size //= radix
        steps.append([i * size for i in range(radix - 1, 0, -1)])
    return steps


def arrivals(value, axis, step):
    return [swap(value, axis, distance) for distance in step]


def join(value, arrived, *beside):
    count = len(arrived)
    done = lax.optimization_barrier((*arrived, *beside))
    return jnp.concatenate([value, *done[:count]], axis=0), *done[count:]


def keys_of(size):
    keys = [0]
    for step in distances_of(size):
        keys = keys + [key ^ distance for distance in step for key in keys]
    return keys


def place_of(mask, keys):
    place, bit = jnp.int32(0), 1
    while bit < len(keys):
        place = place ^ jnp.where((mask & bit) != 0, keys.index(bit), 0)
        bit *= 2
    return place


def id_row(ids, kind, place, me, rows):
    return ids[pl.ds(place * rows + kind * ROUNDS + me, 1), :]


def pick_relations(low, high, table):
    low_column = lax.broadcasted_iota(jnp.int32, (LANES, 1), 0).astype(F32)
    low_hot = (low == low_column).astype(BF16)
    hot = jnp.concatenate(
        [low_hot * (high == float(block)).astype(BF16) for block in range(table.shape[1] // LANES)],
        axis=0,
    )
    columns = jnp.dot(table[...], hot, preferred_element_type=F32).astype(BF16)
    return columns[:, :LANES], columns[:, LANES:]


def pick_blocks(ids, places, me, rows, table, picked):
    for first in range(places.start, places.stop, 2):
        low, high = [
            jnp.concatenate([id_row(ids, kind, place, me, rows) for place in (first, first + 1)], axis=1)
            for kind in (LOW, HIGH)
        ]
        picked[first], picked[first + 1] = pick_relations(low, high, table)


def pack(features, heads, tails, relations):
    rows, width = features.shape

    def placed(value, top, left):
        beyond = rows - top - value.shape[0], width + LANES - left - value.shape[1]
        return lax.pad(value, jnp.zeros((), value.dtype), ((top, beyond[0], 0), (left, beyond[1], 0)))

    kinds = ((HEAD, heads), (TAIL, tails), (HIGH, relations))
    ids = sum(placed(value, kind * ROUNDS, width) for kind, value in kinds)
    both = placed(features, 0, 0).astype(F32) + ids.astype(F32)
    both = lax.optimization_barrier(both)
    ids = both[:, width:]
    high = jnp.floor(ids[HIGH * ROUNDS : LOW * ROUNDS] * (1.0 / LANES))
    low = ids[HIGH * ROUNDS : LOW * ROUNDS] - high * LANES
    ids = jnp.concatenate([ids[: HIGH * ROUNDS], high, low], axis=0)
    return jnp.concatenate([both[:, :width], ids], axis=1).astype(BF16)


def pick_kernel(rows, offset, skipped, stop, block, table, *rest):
    picked, ids = rest[-2:]
    ids[...] = block[:, block.shape[1] - LANES :].astype(F32)
    me = lax.axis_index("grp").astype(jnp.int32)
    count = block.shape[0] // rows
    pick_blocks(ids, range(skipped, stop), me, rows, table, picked.at[pl.ds(offset, count)])


def sigmoid_parts(value):
    small = jnp.exp(-jnp.abs(value))
    softplus = jnp.maximum(value, 0.0) + jnp.log(1.0 + small)
    sigmoid = jnp.where(value >= 0.0, 1.0, small) / (1.0 + small)
    return softplus, sigmoid


def score_kernel(
    rows,
    keys,
    partner,
    mine,
    other,
    w_first,
    w_second,
    table,
    negatives,
    picked_mine,
    picked_early,
    grad_out,
    loss_out,
    slope_out,
    hidden_out,
    encoded,
    ids,
    grads,
    picked_other,
    scores_kept,
    weights_kept,
    partner_kept,
    partner_sem,
):
    fetch = pltpu.make_async_copy(partner, partner_kept, partner_sem)
    fetch.start()
    width = w_first.shape[0]
    half = encoded.shape[1] // 2
    places = len(keys)
    all_rows = places * rows
    group_rows = 2 * rows
    members = (0, all_rows)
    me = lax.axis_index("grp").astype(jnp.int32)

    ids[:all_rows, :] = mine[:, width:].astype(F32)
    ids[all_rows:, :] = other[:, width:].astype(F32)
    features = jnp.concatenate([mine[:, :width], other[:, :width]], axis=0)
    pre_act = jnp.dot(features, w_first[...], preferred_element_type=F32)
    gate = 1.0 / (1.0 + jnp.exp(-pre_act))
    hidden = (pre_act * gate).astype(BF16)
    slope_out[...] = gate * (1.0 + pre_act * (1.0 - gate))
    hidden_out[...] = hidden
    encoded[...] = jnp.dot(hidden, w_second[...], preferred_element_type=F32).astype(BF16).astype(F32)
    early = picked_early.shape[0]
    picked_other[:early] = picked_early[...]
    pick_blocks(ids.at[pl.ds(all_rows, all_rows)], range(early, places), me, rows, table, picked_other)

    labels = [(i ^ (me * rows)).astype(F32) for i in range(group_rows)]
    label_column = lax.broadcasted_iota(jnp.int32, (group_rows, 1), 0) ^ (me * rows)
    drawn = negatives[pl.ds(me, 1), :]
    counts = jnp.sum((drawn == label_column).astype(F32), axis=1, keepdims=True)
    negative_count = negatives.shape[1]
    label_column = label_column.astype(F32)
    fetch.wait()
    far_place = place_of(partner_kept[me, 0], keys)
    low_bit = far_place & -far_place

    def edge_ids(kind, place):
        return jnp.concatenate(
            [id_row(ids.at[pl.ds(base, all_rows)], kind, place, me, rows) for base in members], axis=1
        )

    def group_of(place):
        return jnp.concatenate(
            [encoded[pl.ds(pl.multiple_of(base + place * rows, rows), rows), :] for base in members],
            axis=0,
        )

    def relations_of(place):
        return jnp.concatenate([picked_mine[place], picked_other[place]], axis=1)

    for place in range(places):
        near_rows, far_rows = group_of(place), group_of(place ^ far_place)
        near_re, near_im = near_rows[:, :half], near_rows[:, half:]
        far_re, far_im = far_rows[:, :half], far_rows[:, half:]
        pairs = jnp.concatenate(
            [
                jnp.concatenate(
                    [
                        near_re[i : i + 1] * far_re + near_im[i : i + 1] * far_im,
                        near_re[i : i + 1] * far_im - near_im[i : i + 1] * far_re,
                    ],
                    axis=1,
                ).astype(BF16)
                for i in range(group_rows)
            ],
            axis=0,
        )
        scores = jnp.dot(pairs, relations_of(place), preferred_element_type=F32)
        head = edge_ids(HEAD, place)
        negative = jnp.zeros((group_rows, scores.shape[1]), F32)
        for i in range(group_rows):
            negative = jnp.where(
                head == labels[i], scores[i * group_rows : (i + 1) * group_rows], negative
            )
        scores_kept[place] = negative

    for place in range(places):
        negative = scores_kept[place]
        is_tail = edge_ids(TAIL, place) == label_column
        positive = jnp.sum(jnp.where(is_tail, negative, 0.0), axis=0, keepdims=True)
        loss, chance = sigmoid_parts(negative)
        loss_positive, chance_positive = sigmoid_parts(-positive)
        if place == 0:
            loss_out[...] = loss_positive + jnp.sum(loss * counts, axis=0, keepdims=True) / negative_count
        weight = (chance / negative_count).astype(BF16).astype(F32) * counts
        weights_kept[place] = (weight - jnp.where(is_tail, chance_positive, 0.0)).astype(BF16)

    sublane = lax.broadcasted_iota(jnp.int32, (rows, half), 0)

    def halved(value):
        return value[:rows] + value[rows:]

    def row_sums(blocks):
        step = 1
        while len(blocks) > 1:
            upper = (sublane & step) != 0
            blocks = [
                jnp.where(upper, second, first) + pltpu.roll(jnp.where(upper, first, second), step, 0)
                for first, second in zip(blocks[::2], blocks[1::2], strict=True)
            ]
            step *= 2
        return blocks[0]

    for pair in range(places // 2):
        place = pair + (pair & -low_bit)
        far = place ^ far_place
        near_weight, far_weight = weights_kept[place], weights_kept[far]
        near_head, far_head = edge_ids(HEAD, place), edge_ids(HEAD, far)
        far_hot = (far_head == label_column).astype(BF16)
        near_rows, far_rows = group_of(place), group_of(far)
        near_re, near_im = near_rows[:, :half], near_rows[:, half:]
        far_re, far_im = far_rows[:, :half], far_rows[:, half:]
        weights = jnp.concatenate(
            [
                jnp.concatenate(
                    [near_weight * (near_head == labels[i]).astype(BF16), far_weight[i : i + 1] * far_hot],
                    axis=1,
                )
                for i in range(group_rows)
            ],
            axis=0,
        )
        relation = relations_of(place)
        relation = jnp.concatenate([relation[:half], -relation[half:]], axis=0)
        joint = lax.dot_general(
            weights,
            jnp.concatenate([relation, relations_of(far)], axis=1),
            (((1,), (1,)), ((), ())),
            preferred_element_type=F32,
        )
        far_grad_re = jnp.zeros((group_rows, half), F32)
        far_grad_im = jnp.zeros((group_rows, half), F32)
        near_grad = []
        for i in range(group_rows):
            part_re = joint[i * group_rows : (i + 1) * group_rows, :half]
            part_im = joint[i * group_rows : (i + 1) * group_rows, half:]
            row_re, row_im = near_re[i : i + 1], near_im[i : i + 1]
            far_grad_re = far_grad_re + (row_re * part_re + row_im * part_im)
            far_grad_im = far_grad_im + (row_im * part_re - row_re * part_im)
            near_grad.append(
                (
                    halved(far_re * part_re - far_im * part_im),
                    halved(far_im * part_re + far_re * part_im),
                )
            )
        near_grad = jnp.concatenate(
            [
                jnp.concatenate([row_sums([part[k] for part in near_grad[i : i + rows]]) for k in (0, 1)], axis=1)
                for i in range(0, group_rows, rows)
            ],
            axis=0,
        )
        far_grad = jnp.concatenate([far_grad_re, far_grad_im], axis=1)
        for member, base in enumerate(members):
            span = slice(member * rows, (member + 1) * rows)
            grads[pl.ds(pl.multiple_of(base + place * rows, rows), rows), :] = near_grad[span]
            grads[pl.ds(pl.multiple_of(base + far * rows, rows), rows), :] = far_grad[span]
    grad_out[...] = grads[...].astype(BF16)


def total_kernel(
    limit,
    mine,
    other,
    grad_mine,
    grad_other,
    slope,
    hidden,
    w_second,
    loss_mine,
    loss_other,
    loss_out,
    first_out,
    second_out,
):
    me = lax.axis_index("grp").astype(jnp.int32)
    all_rows = mine.shape[0]
    grad = jnp.concatenate(
        [
            grad_mine[:all_rows].astype(F32) + grad_other[all_rows:].astype(F32),
            grad_mine[all_rows:].astype(F32) + grad_other[:all_rows].astype(F32),
        ],
        axis=0,
    ).astype(BF16)
    across = (((0,), (0,)), ((), ()))
    grad_hidden = lax.dot_general(
        grad, w_second[...], (((1,), (1,)), ((), ())), preferred_element_type=F32
    )
    grad_pre = (grad_hidden * slope[...]).astype(BF16)
    squares = jnp.zeros((1, 1), F32)
    for target, parts, factor in ((second_out, (hidden,), grad), (first_out, (mine, other), grad_pre)):
        share = target.shape[0]
        for member in (me, 1 - me):
            columns = pl.ds(pl.multiple_of(member * share, share), share)
            rows = jnp.concatenate([part[:, columns] for part in parts], axis=0)
            total = lax.dot_general(rows, factor, across, preferred_element_type=F32)
            squares = squares + jnp.sum(total * total, axis=(0, 1), keepdims=True)
            if member is me:
                target[...] = total
    factor = jnp.minimum(1.0, limit / jnp.sqrt(squares + 1e-06))
    first_out[...] = first_out[...] * factor
    second_out[...] = second_out[...] * factor
    edges = loss_out.shape[1]
    for member in range(2):
        loss_out[pl.ds(member, 1), :] = jnp.where(
            me == member, loss_mine[:, :edges], loss_other[:, edges:]
        )


def kernel_call(body, name, out_shape, scratch=(), flops=0, spaces=None, mebibytes=20, **more):
    vmem = pl.BlockSpec(memory_space=pltpu.VMEM)
    in_specs = None if spaces is None else [pl.BlockSpec(memory_space=space) for space in spaces]
    return pl.pallas_call(
        body,
        out_shape=out_shape,
        in_specs=in_specs,
        out_specs=jax.tree.map(lambda _: vmem, out_shape),
        scratch_shapes=scratch,
        compiler_params=pltpu.CompilerParams(vmem_limit_bytes=mebibytes * 1024 * 1024),
        cost_estimate=pl.CostEstimate(flops=flops, bytes_accessed=0, transcendentals=0),
        name=name,
        **more,
    )


def together(
    features, w_first, w_second, relation_table, heads, relations, tails, negatives, partner
):
    rows, width = features.shape
    rounds, edges = heads.shape
    hidden_width, encoded_width = w_second.shape
    size = lax.axis_size("dom")
    keys = keys_of(size)
    steps = distances_of(size)
    all_rows = 2 * size * rows
    shape = jax.ShapeDtypeStruct
    table = jnp.pad(relation_table.T, ((0, 0), (0, -relation_table.shape[0] % LANES)))
    picked_shape = shape((size, encoded_width, edges), BF16)
    flops = 2 * table.size * edges

    block = pack(features, heads, tails, relations)
    for step in steps[:-1]:
        block, table = join(block, arrivals(block, "dom", step), table)
    early = block.shape[0] // rows

    def pick(block, count, *begun, offset=0, skipped=0, stop=None):
        places = block.shape[0] // rows
        stop = places if stop is None else stop
        return kernel_call(
            functools.partial(pick_kernel, rows, offset, skipped, stop),
            "pick",
            shape((count, encoded_width, edges), BF16),
            [pltpu.VMEM((places * rows, edges), F32)],
            flops * (stop - skipped),
            [pltpu.VMEM] * (2 + len(begun)),
            input_output_aliases={2: 0} if begun else {},
        )(block, table, *begun)

    early_ids = swap(block[:, width:], "grp", 1)
    arrived = arrivals(block, "dom", steps[-1])
    picked = pick(block, size)
    picked_early = pick(early_ids, early)
    picked = pick(arrived[0], size, picked, offset=early)
    done = 2 * early
    if len(arrived) > 1:
        picked = pick(arrived[1], size, picked, offset=done, stop=early // 2)
        done += early // 2
    mine, picked, picked_early = join(block, arrived, picked, picked_early)
    picked = pick(mine, size, picked, skipped=done)
    other = swap(mine, "grp", 1)

    grad, loss, slope, hidden = kernel_call(
        functools.partial(score_kernel, rows, keys),
        "scores",
        (
            shape((all_rows, encoded_width), BF16),
            shape((1, 2 * edges), F32),
            shape((all_rows, hidden_width), F32),
            shape((all_rows, hidden_width), BF16),
        ),
        [
            pltpu.VMEM((all_rows, encoded_width), F32),
            pltpu.VMEM((all_rows, edges), F32),
            pltpu.VMEM((all_rows, encoded_width), F32),
            pltpu.VMEM(picked_shape.shape, BF16),
            pltpu.VMEM((size, 2 * rows, 2 * edges), F32),
            pltpu.VMEM((size, 2 * rows, 2 * edges), BF16),
            pltpu.SMEM(partner.shape, jnp.int32),
            pltpu.SemaphoreType.DMA,
        ],
        flops * size * 2,
        [pl.ANY] + [pltpu.VMEM] * 8,
    )(partner, mine, other, w_first, w_second, table, negatives, picked, picked_early)
    grad_other = swap(grad, "grp", 1)
    loss_other = swap(loss, "grp", 1)
    return kernel_call(
        functools.partial(total_kernel, math.sqrt(w_first.size + w_second.size)),
        "totals",
        (
            shape((rounds, edges), F32),
            shape((w_first.shape[0] // 2, w_first.shape[1]), F32),
            shape((w_second.shape[0] // 2, w_second.shape[1]), F32),
        ),
        spaces=[pltpu.VMEM] * 9,
    )(mine, other, grad, grad_other, slope, hidden, w_second, loss, loss_other)


def solution(mesh):
    def per_device(features, w_first, w_second, relation_table, heads, relations, tails, *rest):
        rounds, edges = heads.shape
        rows = features.shape[0]
        fits = (
            mesh.shape["grp"] == rounds == ROUNDS == 2
            and edges == LANES
            and 4 * rounds == rows
            and mesh.shape["dom"] >= 8
            and relation_table.shape[0] <= LANES * 256
        )
        plan = together if fits else spread
        return plan(features, w_first, w_second, relation_table, heads, relations, tails, *rest)

    return jax.shard_map(
        per_device,
        mesh=mesh,
        in_specs=(
            P(("dom", "grp"), None),
            P(),
            P(),
            P(),
            P(None, ("dom", "grp")),
            P(None, ("dom", "grp")),
            P(None, ("dom", "grp")),
            P(),
            P(),
        ),
        out_specs=(P(None, ("dom", "grp")), P("grp", None), P("grp", None)),
        check_vma=False,
    )
```

```python
import functools
import math

import jax
import jax.numpy as jnp
from jax import lax
from jax.experimental import pallas as pl
from jax.experimental.pallas import tpu as pltpu
from jax.sharding import PartitionSpec as P

LANES = 128
F32 = jnp.float32
BF16 = jnp.bfloat16


def partner_2(value, axis, distance):
    return lax.ppermute(value, axis, [(i, i ^ 1 << distance) for i in range(lax.axis_size(axis))])


def encode(rows, w_first, w_second):
    pre_act = jnp.dot(rows, w_first, preferred_element_type=jnp.float32)
    hidden = jax.nn.silu(pre_act).astype(jnp.bfloat16)
    encoded = jnp.dot(hidden, w_second, preferred_element_type=jnp.float32).astype(jnp.bfloat16)
    return (pre_act, hidden, encoded)


def backward(rows, pre_act, hidden, grad_rows, w_second):
    term_second = lax.dot_general(
        hidden, grad_rows, (((0,), (0,)), ((), ())), preferred_element_type=jnp.float32
    )
    grad_hidden = lax.dot_general(
        grad_rows, w_second, (((1,), (1,)), ((), ())), preferred_element_type=jnp.float32
    )
    sigmoid_pre = jax.nn.sigmoid(pre_act)
    silu_slope = sigmoid_pre * (1.0 + pre_act * (1.0 - sigmoid_pre))
    grad_pre = (grad_hidden * silu_slope).astype(jnp.bfloat16)
    term_first = lax.dot_general(
        rows, grad_pre, (((0,), (0,)), ((), ())), preferred_element_type=jnp.float32
    )
    return (term_first, term_second)


def row_select(ids, row_count):
    return ids[:, None] == jnp.arange(row_count, dtype=jnp.int32)[None, :]


def pick_rows(selector, table):
    return jnp.dot(selector.astype(jnp.bfloat16), table, preferred_element_type=jnp.float32)


def add_into_rows(selector, values):
    return lax.dot_general(
        selector.astype(jnp.float32),
        values,
        (((0,), (0,)), ((), ())),
        precision=lax.Precision.HIGHEST,
        preferred_element_type=jnp.float32,
    )


def score_block(own, other, relation_table, head_ids, relation_ids, tail_ids, negative_ids):
    half_width = own.shape[1] // 2
    row_count = own.shape[0]
    head_select = row_select(head_ids, row_count)
    tail_select = row_select(tail_ids, row_count)
    negative_select = row_select(negative_ids, row_count)
    head_rows = pick_rows(head_select, own)
    rel_rows = jnp.take(relation_table, relation_ids, axis=0).astype(jnp.float32)
    tail_rows = pick_rows(tail_select, other)
    negative_rows = pick_rows(negative_select, other).astype(jnp.bfloat16)
    head_real, head_imag = (head_rows[:, :half_width], head_rows[:, half_width:])
    rel_real, rel_imag = (rel_rows[:, :half_width], rel_rows[:, half_width:])
    query = jnp.concatenate(
        [head_real * rel_real - head_imag * rel_imag, head_real * rel_imag + head_imag * rel_real],
        axis=1,
    ).astype(jnp.bfloat16)
    query_wide = query.astype(jnp.float32)
    positive = jnp.sum(query_wide * tail_rows, axis=1)
    negative = lax.dot_general(
        query, negative_rows, (((1,), (1,)), ((), ())), preferred_element_type=jnp.float32
    )
    edge_loss = (
        jax.nn.softplus(-positive) + jnp.sum(jax.nn.softplus(negative), axis=1) / negative.shape[1]
    )
    weight_neg = (jax.nn.sigmoid(negative) / negative.shape[1]).astype(jnp.bfloat16)
    weight_pos = -jax.nn.sigmoid(-positive)
    grad_query = weight_pos[:, None] * tail_rows + jnp.dot(
        weight_neg, negative_rows, preferred_element_type=jnp.float32
    )
    grad_tail = weight_pos[:, None] * query_wide
    grad_negative = lax.dot_general(
        weight_neg, query, (((0,), (0,)), ((), ())), preferred_element_type=jnp.float32
    )
    grad_real, grad_imag = (grad_query[:, :half_width], grad_query[:, half_width:])
    grad_head = jnp.concatenate(
        [grad_real * rel_real + grad_imag * rel_imag, grad_imag * rel_real - grad_real * rel_imag],
        axis=1,
    )
    own_part = add_into_rows(head_select, grad_head)
    far_part = add_into_rows(tail_select, grad_tail) + add_into_rows(negative_select, grad_negative)
    return (edge_loss, own_part, far_part)


def route_rows(payload, xor_mask, bit_count, mover):
    for bit_level in range(bit_count):
        swapped = mover(payload, bit_level)
        payload = jnp.where(xor_mask >> bit_level & 1 == 1, swapped, payload)
    return payload


def spread(
    features, w_first, w_second, relation_table, heads, relations, tails, negatives, partner
):
    pre_act, hidden, encoded = encode(features, w_first, w_second)
    own_block = lax.all_gather(encoded, "grp", axis=0, tiled=True)
    bit_count = lax.axis_size("dom").bit_length() - 1
    total_first = jnp.zeros(w_first.shape, jnp.float32)
    total_second = jnp.zeros(w_second.shape, jnp.float32)
    own_acc = jnp.zeros(own_block.shape, jnp.float32)
    losses = []
    for bucket in range(heads.shape[0]):
        xor_mask = partner[bucket, 0]
        arrived = route_rows(
            encoded,
            xor_mask,
            bit_count,
            lambda payload, bit_level: partner_2(payload, "dom", bit_level),
        )
        far_block = lax.all_gather(arrived, "grp", axis=0, tiled=True)
        edge_loss, own_part, far_part = score_block(
            own_block,
            far_block,
            relation_table,
            heads[bucket],
            relations[bucket],
            tails[bucket],
            negatives[bucket],
        )
        losses.append(edge_loss)
        own_acc = own_acc + own_part
        far_grad = lax.psum_scatter(
            far_part.astype(jnp.bfloat16), "grp", scatter_dimension=0, tiled=True
        )
        returned = route_rows(
            far_grad,
            xor_mask,
            bit_count,
            lambda payload, bit_level: partner_2(payload, "dom", bit_level),
        )
        term_first, term_second = backward(features, pre_act, hidden, returned, w_second)
        total_first = total_first + term_first
        total_second = total_second + term_second
    own_grad = lax.psum_scatter(
        own_acc.astype(jnp.bfloat16), "grp", scatter_dimension=0, tiled=True
    )
    term_first, term_second = backward(features, pre_act, hidden, own_grad, w_second)
    total_first = total_first + term_first
    total_second = total_second + term_second
    part_first, part_second = (
        lax.psum_scatter(
            total_first.astype(jnp.bfloat16), "grp", scatter_dimension=0, tiled=True
        ).astype(jnp.float32),
        lax.psum_scatter(
            total_second.astype(jnp.bfloat16), "grp", scatter_dimension=0, tiled=True
        ).astype(jnp.float32),
    )
    summed_first, summed_second = lax.psum((part_first, part_second), "dom")
    local_squares = jnp.sum(summed_first * summed_first) + jnp.sum(summed_second * summed_second)
    squares = lax.psum(local_squares, "grp")
    factor = jnp.minimum(1.0, math.sqrt(w_first.size + w_second.size) / jnp.sqrt(squares + 1e-06))
    return (jnp.stack(losses), summed_first * factor, summed_second * factor)


ROUNDS = 2
HEAD, TAIL, HIGH, LOW = 0, 1, 2, 3
LANE_BITS = LANES.bit_length() - 1


def swap(value, axis, distance):
    return lax.ppermute(value, axis, [(i, i ^ distance) for i in range(lax.axis_size(axis))])


def distances_of(size):
    bits = [1 << i for i in reversed(range(size.bit_length() - 1))]
    steps = []
    while bits:
        step = [bits.pop(0)]
        if bits:
            step.append(bits.pop(len(bits) // 2))
            step.insert(0, sum(step))
        steps.append(step)
    return steps


def arrivals(value, axis, step):
    return [swap(value, axis, distance) for distance in step]


def join(value, arrived, *beside):
    count = len(arrived)
    done = lax.optimization_barrier((*arrived, *beside))
    return jnp.concatenate([value, *done[:count]], axis=0), *done[count:]


def keys_of(size):
    keys = [0]
    for step in distances_of(size):
        keys = keys + [key ^ distance for distance in step for key in keys]
    return keys


def place_of(mask, keys):
    place, bit = jnp.int32(0), 1
    while bit < len(keys):
        place = place ^ jnp.where((mask & bit) != 0, keys.index(bit), 0)
        bit *= 2
    return place


def id_row(ids, kind, place, me, rows):
    return ids[pl.ds(place * rows + kind * ROUNDS + me, 1), :]


def pick_relations(low, high, table):
    low_column = lax.broadcasted_iota(jnp.int32, (LANES, 1), 0).astype(F32)
    low_hot = (low == low_column).astype(BF16)
    hot = jnp.concatenate(
        [low_hot * (high == float(block)).astype(BF16) for block in range(table.shape[1] // LANES)],
        axis=0,
    )
    columns = jnp.dot(table[...], hot, preferred_element_type=F32).astype(BF16)
    return columns[:, :LANES], columns[:, LANES:]


def pick_blocks(ids, places, me, rows, table, picked):
    for first in range(places.start, places.stop, 2):
        low, high = [
            jnp.concatenate([id_row(ids, kind, place, me, rows) for place in (first, first + 1)], axis=1)
            for kind in (LOW, HIGH)
        ]
        picked[first], picked[first + 1] = pick_relations(low, high, table)


def pack(features, heads, tails, relations):
    rows, width = features.shape

    def placed(value, top, left):
        beyond = rows - top - value.shape[0], width + LANES - left - value.shape[1]
        return lax.pad(value, jnp.zeros((), value.dtype), ((top, beyond[0], 0), (left, beyond[1], 0)))

    kinds = ((HEAD, heads), (TAIL, tails), (HIGH, relations))
    ids = sum(placed(value, kind * ROUNDS, width) for kind, value in kinds)
    both = placed(features, 0, 0).astype(F32) + ids.astype(F32)
    both = lax.optimization_barrier(both)
    ids = both[:, width:]
    high = jnp.floor(ids[HIGH * ROUNDS : LOW * ROUNDS] * (1.0 / LANES))
    low = ids[HIGH * ROUNDS : LOW * ROUNDS] - high * LANES
    ids = jnp.concatenate([ids[: HIGH * ROUNDS], high, low], axis=0)
    return jnp.concatenate([both[:, :width], ids], axis=1).astype(BF16)


def pick_kernel(rows, offset, skipped, stop, block, table, *rest):
    picked, ids = rest[-2:]
    ids[...] = block[:, block.shape[1] - LANES :].astype(F32)
    me = lax.axis_index("grp").astype(jnp.int32)
    count = block.shape[0] // rows
    pick_blocks(ids, range(skipped, stop), me, rows, table, picked.at[pl.ds(offset, count)])


def sigmoid_parts(value):
    small = jnp.exp(-jnp.abs(value))
    softplus = jnp.maximum(value, 0.0) + jnp.log(1.0 + small)
    sigmoid = jnp.where(value >= 0.0, 1.0, small) / (1.0 + small)
    return softplus, sigmoid


def score_kernel(
    rows,
    keys,
    partner,
    mine,
    other,
    w_first,
    w_second,
    table,
    negatives,
    picked_mine,
    picked_early,
    grad_out,
    loss_out,
    slope_out,
    hidden_out,
    encoded,
    ids,
    grads,
    picked_other,
    scores_kept,
    weights_kept,
    partner_kept,
    partner_sem,
):
    fetch = pltpu.make_async_copy(partner, partner_kept, partner_sem)
    fetch.start()
    width = w_first.shape[0]
    half = encoded.shape[1] // 2
    places = len(keys)
    all_rows = places * rows
    group_rows = 2 * rows
    members = (0, all_rows)
    me = lax.axis_index("grp").astype(jnp.int32)

    ids[:all_rows, :] = mine[:, width:].astype(F32)
    ids[all_rows:, :] = other[:, width:].astype(F32)
    features = jnp.concatenate([mine[:, :width], other[:, :width]], axis=0)
    pre_act = jnp.dot(features, w_first[...], preferred_element_type=F32)
    gate = 1.0 / (1.0 + jnp.exp(-pre_act))
    hidden = (pre_act * gate).astype(BF16)
    slope_out[...] = gate * (1.0 + pre_act * (1.0 - gate))
    hidden_out[...] = hidden
    encoded[...] = jnp.dot(hidden, w_second[...], preferred_element_type=F32).astype(BF16).astype(F32)
    early = picked_early.shape[0]
    picked_other[:early] = picked_early[...]
    pick_blocks(ids.at[pl.ds(all_rows, all_rows)], range(early, places), me, rows, table, picked_other)

    labels = [(i ^ (me * rows)).astype(F32) for i in range(group_rows)]
    label_column = lax.broadcasted_iota(jnp.int32, (group_rows, 1), 0) ^ (me * rows)
    drawn = negatives[pl.ds(me, 1), :]
    counts = jnp.sum((drawn == label_column).astype(F32), axis=1, keepdims=True)
    negative_count = negatives.shape[1]
    label_column = label_column.astype(F32)
    fetch.wait()
    far_place = place_of(partner_kept[me, 0], keys)
    low_bit = far_place & -far_place

    def edge_ids(kind, place):
        return jnp.concatenate(
            [id_row(ids.at[pl.ds(base, all_rows)], kind, place, me, rows) for base in members], axis=1
        )

    def group_of(place):
        return jnp.concatenate(
            [encoded[pl.ds(pl.multiple_of(base + place * rows, rows), rows), :] for base in members],
            axis=0,
        )

    def relations_of(place):
        return jnp.concatenate([picked_mine[place], picked_other[place]], axis=1)

    for place in range(places):
        near_rows, far_rows = group_of(place), group_of(place ^ far_place)
        near_re, near_im = near_rows[:, :half], near_rows[:, half:]
        far_re, far_im = far_rows[:, :half], far_rows[:, half:]
        pairs = jnp.concatenate(
            [
                jnp.concatenate(
                    [
                        near_re[i : i + 1] * far_re + near_im[i : i + 1] * far_im,
                        near_re[i : i + 1] * far_im - near_im[i : i + 1] * far_re,
                    ],
                    axis=1,
                ).astype(BF16)
                for i in range(group_rows)
            ],
            axis=0,
        )
        scores = jnp.dot(pairs, relations_of(place), preferred_element_type=F32)
        head = edge_ids(HEAD, place)
        negative = jnp.zeros((group_rows, scores.shape[1]), F32)
        for i in range(group_rows):
            negative = jnp.where(
                head == labels[i], scores[i * group_rows : (i + 1) * group_rows], negative
            )
        scores_kept[place] = negative

    for place in range(places):
        negative = scores_kept[place]
        is_tail = edge_ids(TAIL, place) == label_column
        positive = jnp.sum(jnp.where(is_tail, negative, 0.0), axis=0, keepdims=True)
        loss, chance = sigmoid_parts(negative)
        loss_positive, chance_positive = sigmoid_parts(-positive)
        if place == 0:
            loss_out[...] = loss_positive + jnp.sum(loss * counts, axis=0, keepdims=True) / negative_count
        weight = (chance / negative_count).astype(BF16).astype(F32) * counts
        weights_kept[place] = (weight - jnp.where(is_tail, chance_positive, 0.0)).astype(BF16)

    sublane = lax.broadcasted_iota(jnp.int32, (rows, half), 0)

    def halved(value):
        return value[:rows] + value[rows:]

    def row_sums(blocks):
        step = 1
        while len(blocks) > 1:
            upper = (sublane & step) != 0
            blocks = [
                jnp.where(upper, second, first) + pltpu.roll(jnp.where(upper, first, second), step, 0)
                for first, second in zip(blocks[::2], blocks[1::2], strict=True)
            ]
            step *= 2
        return blocks[0]

    for pair in range(places // 2):
        place = pair + (pair & -low_bit)
        far = place ^ far_place
        near_weight, far_weight = weights_kept[place], weights_kept[far]
        near_head, far_head = edge_ids(HEAD, place), edge_ids(HEAD, far)
        far_hot = (far_head == label_column).astype(BF16)
        near_rows, far_rows = group_of(place), group_of(far)
        near_re, near_im = near_rows[:, :half], near_rows[:, half:]
        far_re, far_im = far_rows[:, :half], far_rows[:, half:]
        weights = jnp.concatenate(
            [
                jnp.concatenate(
                    [near_weight * (near_head == labels[i]).astype(BF16), far_weight[i : i + 1] * far_hot],
                    axis=1,
                )
                for i in range(group_rows)
            ],
            axis=0,
        )
        relation = relations_of(place)
        relation = jnp.concatenate([relation[:half], -relation[half:]], axis=0)
        joint = lax.dot_general(
            weights,
            jnp.concatenate([relation, relations_of(far)], axis=1),
            (((1,), (1,)), ((), ())),
            preferred_element_type=F32,
        )
        far_grad_re = jnp.zeros((group_rows, half), F32)
        far_grad_im = jnp.zeros((group_rows, half), F32)
        near_grad = []
        for i in range(group_rows):
            part_re = joint[i * group_rows : (i + 1) * group_rows, :half]
            part_im = joint[i * group_rows : (i + 1) * group_rows, half:]
            row_re, row_im = near_re[i : i + 1], near_im[i : i + 1]
            far_grad_re = far_grad_re + (row_re * part_re + row_im * part_im)
            far_grad_im = far_grad_im + (row_im * part_re - row_re * part_im)
            near_grad.append(
                (
                    halved(far_re * part_re - far_im * part_im),
                    halved(far_im * part_re + far_re * part_im),
                )
            )
        near_grad = jnp.concatenate(
            [
                jnp.concatenate([row_sums([part[k] for part in near_grad[i : i + rows]]) for k in (0, 1)], axis=1)
                for i in range(0, group_rows, rows)
            ],
            axis=0,
        )
        far_grad = jnp.concatenate([far_grad_re, far_grad_im], axis=1)
        for member, base in enumerate(members):
            span = slice(member * rows, (member + 1) * rows)
            grads[pl.ds(pl.multiple_of(base + place * rows, rows), rows), :] = near_grad[span]
            grads[pl.ds(pl.multiple_of(base + far * rows, rows), rows), :] = far_grad[span]
    grad_out[...] = grads[...].astype(BF16)


def total_kernel(
    limit,
    mine,
    other,
    grad_mine,
    grad_other,
    slope,
    hidden,
    w_second,
    loss_mine,
    loss_other,
    loss_out,
    first_out,
    second_out,
):
    me = lax.axis_index("grp").astype(jnp.int32)
    all_rows = mine.shape[0]
    grad = jnp.concatenate(
        [
            grad_mine[:all_rows].astype(F32) + grad_other[all_rows:].astype(F32),
            grad_mine[all_rows:].astype(F32) + grad_other[:all_rows].astype(F32),
        ],
        axis=0,
    ).astype(BF16)
    across = (((0,), (0,)), ((), ()))
    grad_hidden = lax.dot_general(
        grad, w_second[...], (((1,), (1,)), ((), ())), preferred_element_type=F32
    )
    grad_pre = (grad_hidden * slope[...]).astype(BF16)
    squares = jnp.zeros((1, 1), F32)
    for target, parts, factor in ((second_out, (hidden,), grad), (first_out, (mine, other), grad_pre)):
        share = target.shape[0]
        for member in (me, 1 - me):
            columns = pl.ds(pl.multiple_of(member * share, share), share)
            rows = jnp.concatenate([part[:, columns] for part in parts], axis=0)
            total = lax.dot_general(rows, factor, across, preferred_element_type=F32)
            squares = squares + jnp.sum(total * total, axis=(0, 1), keepdims=True)
            if member is me:
                target[...] = total
    factor = jnp.minimum(1.0, limit / jnp.sqrt(squares + 1e-06))
    first_out[...] = first_out[...] * factor
    second_out[...] = second_out[...] * factor
    edges = loss_out.shape[1]
    for member in range(2):
        loss_out[pl.ds(member, 1), :] = jnp.where(
            me == member, loss_mine[:, :edges], loss_other[:, edges:]
        )


def kernel_call(body, name, out_shape, scratch=(), flops=0, spaces=None, mebibytes=20, **more):
    vmem = pl.BlockSpec(memory_space=pltpu.VMEM)
    in_specs = None if spaces is None else [pl.BlockSpec(memory_space=space) for space in spaces]
    return pl.pallas_call(
        body,
        out_shape=out_shape,
        in_specs=in_specs,
        out_specs=jax.tree.map(lambda _: vmem, out_shape),
        scratch_shapes=scratch,
        compiler_params=pltpu.CompilerParams(vmem_limit_bytes=mebibytes * 1024 * 1024),
        cost_estimate=pl.CostEstimate(flops=flops, bytes_accessed=0, transcendentals=0),
        name=name,
        **more,
    )


def together(
    features, w_first, w_second, relation_table, heads, relations, tails, negatives, partner
):
    rows, width = features.shape
    rounds, edges = heads.shape
    hidden_width, encoded_width = w_second.shape
    size = lax.axis_size("dom")
    keys = keys_of(size)
    steps = distances_of(size)
    all_rows = 2 * size * rows
    shape = jax.ShapeDtypeStruct
    table = jnp.pad(relation_table.T, ((0, 0), (0, -relation_table.shape[0] % LANES)))
    picked_shape = shape((size, encoded_width, edges), BF16)
    flops = 2 * table.size * edges

    block = pack(features, heads, tails, relations)
    for step in steps[:-1]:
        block, table = join(block, arrivals(block, "dom", step), table)
    early = block.shape[0] // rows

    def pick(block, count, *begun, offset=0, skipped=0, stop=None):
        places = block.shape[0] // rows
        stop = places if stop is None else stop
        return kernel_call(
            functools.partial(pick_kernel, rows, offset, skipped, stop),
            "pick",
            shape((count, encoded_width, edges), BF16),
            [pltpu.VMEM((places * rows, edges), F32)],
            flops * (stop - skipped),
            [pltpu.VMEM] * (2 + len(begun)),
            input_output_aliases={2: 0} if begun else {},
        )(block, table, *begun)

    early_ids = swap(block[:, width:], "grp", 1)
    arrived = arrivals(block, "dom", steps[-1])
    picked = pick(block, size)
    picked_early = pick(early_ids, early)
    picked = pick(arrived[0], size, picked, offset=early)
    done = 2 * early
    if len(arrived) > 1:
        picked = pick(arrived[1], size, picked, offset=done, stop=early // 2)
        done += early // 2
    mine, picked, picked_early = join(block, arrived, picked, picked_early)
    picked = pick(mine, size, picked, skipped=done)
    other = swap(mine, "grp", 1)

    grad, loss, slope, hidden = kernel_call(
        functools.partial(score_kernel, rows, keys),
        "scores",
        (
            shape((all_rows, encoded_width), BF16),
            shape((1, 2 * edges), F32),
            shape((all_rows, hidden_width), F32),
            shape((all_rows, hidden_width), BF16),
        ),
        [
            pltpu.VMEM((all_rows, encoded_width), F32),
            pltpu.VMEM((all_rows, edges), F32),
            pltpu.VMEM((all_rows, encoded_width), F32),
            pltpu.VMEM(picked_shape.shape, BF16),
            pltpu.VMEM((size, 2 * rows, 2 * edges), F32),
            pltpu.VMEM((size, 2 * rows, 2 * edges), BF16),
            pltpu.SMEM(partner.shape, jnp.int32),
            pltpu.SemaphoreType.DMA,
        ],
        flops * size * 2,
        [pl.ANY] + [pltpu.VMEM] * 8,
    )(partner, mine, other, w_first, w_second, table, negatives, picked, picked_early)
    grad_other = swap(grad, "grp", 1)
    loss_other = swap(loss, "grp", 1)
    return kernel_call(
        functools.partial(total_kernel, math.sqrt(w_first.size + w_second.size)),
        "totals",
        (
            shape((rounds, edges), F32),
            shape((w_first.shape[0] // 2, w_first.shape[1]), F32),
            shape((w_second.shape[0] // 2, w_second.shape[1]), F32),
        ),
        spaces=[pltpu.VMEM] * 9,
    )(mine, other, grad, grad_other, slope, hidden, w_second, loss, loss_other)


def solution(mesh):
    def per_device(features, w_first, w_second, relation_table, heads, relations, tails, *rest):
        rounds, edges = heads.shape
        rows = features.shape[0]
        fits = (
            mesh.shape["grp"] == rounds == ROUNDS == 2
            and edges == LANES
            and 4 * rounds == rows
            and mesh.shape["dom"] >= 8
            and relation_table.shape[0] <= LANES * 256
        )
        plan = together if fits else spread
        return plan(features, w_first, w_second, relation_table, heads, relations, tails, *rest)

    return jax.shard_map(
        per_device,
        mesh=mesh,
        in_specs=(
            P(("dom", "grp"), None),
            P(),
            P(),
            P(),
            P(None, ("dom", "grp")),
            P(None, ("dom", "grp")),
            P(None, ("dom", "grp")),
            P(),
            P(),
        ),
        out_specs=(P(None, ("dom", "grp")), P("grp", None), P("grp", None)),
        check_vma=False,
    )
```
